32 devices in a mesh: ep: 8 (over z, y), sp: 4 (over x, core).
Axes of the slice: x: 2, y: 2, z: 4, core: 2. Of those that a mesh axis runs over, the one named last changes fastest.
Arguments:
- tokens: bfloat16 [4096, 2048], P(('sp', 'ep')), parts along dimension 0, may hold values from -6 to 6
- norm_gain: float32 [2048], replicated, may hold values from 0.1 to 1.9
- expert_ids: int32 [4096, 8], P(('sp', 'ep')), parts along dimension 0, may hold values from 0 to 127, all different within a row; in each aligned block of 128 rows (0 to 127, 128 to 255, ...) at most 16 rows name the same one
- gate_vals: float32 [4096, 8], P(('sp', 'ep')), parts along dimension 0, may hold values from 0.25 to 4
- live_counts: int32 [32], P(('sp', 'ep')), parts along dimension 0, may hold values from 1 to 128, 896 in all
- w_gate: bfloat16 [2048, 1536], P(None, 'ep'), may hold values from -0.125 to 0.125
- w_up: bfloat16 [2048, 1536], P(None, 'ep'), may hold values from -0.125 to 0.125
- w_down: bfloat16 [1536, 2048], P('ep'), may hold values from -0.15625 to 0.15625
Outputs:
- moe_out: bfloat16 [4096, 2048], P(('sp', 'ep')), parts along dimension 0
The draws below stay inside these ranges and needn't reach their ends.
There are 4 independent parts, one for each index of `sp`. The reference program is written for one: setup_inputs(seed, part) draws one part's arguments, and reference() takes and returns one part's arrays. A program takes and returns all parts, laid end to end along the dimension named above; an argument that names none is the same for every part. Nothing has to cross between parts.
Inputs may be any that keep to these rules, and one draw needn't show every extreme that they name: `expert_ids`: each row names 8 different experts. Within the rows of one device no expert is named by more than 16 rows, a bound that some block reaches. `live_counts`: they sum to 896; one device is full.
All inputs are finite; a program needn't handle non-finite values.
Results may differ from the reference program's by a relative error of at most 0.0089.
Values may be sent and summed in bfloat16 or wider, within the bound.
No kernel may reach another device: no remote copies, remote signals or barrier semaphores. Data moves between devices by JAX's collectives and lax.ppermute only.
A program may use at most 64 MiB of HBM per device.

```python
import math
import jax
import jax.numpy as jnp
import numpy as np
from jax import lax

D = 2048
H = 1536
EXPERTS = 128
TOPK = 8
SLICES = 8
TOK_DEV = 128
CAP = 16
FLIGHT = 1
TOKENS = 1024
N_EP = 8


def shard_levels(stream_key, extent, cuts, smallest, top_value):
    factor_of = 1.0
    for axis_at, parts in cuts:
        steps = jax.random.uniform(jax.random.fold_in(jax.random.fold_in(stream_key, 6), axis_at), (parts,), jnp.float32, smallest / len(cuts), top_value / len(cuts))
        factor_of = factor_of * jnp.repeat(jnp.exp(steps), extent[axis_at] // parts).reshape((-1,) + (1,) * (len(extent) - 1 - axis_at))
    return factor_of


def profile(amount, total, most, skew):
    loads = [(1 << 20) // math.isqrt(rank ** skew) + 1 for rank in range(2, amount + 1)]
    surplus, holding = total - most - (amount - 1), [1] * (amount - 1)
    while surplus > 0:
        candidates = [i for i in range(amount - 1) if holding[i] < most]
        pool, left = sum([loads[i] for i in candidates]), surplus
        for i in candidates:
            addition = min(most - holding[i], max(1, left * loads[i] // pool), surplus)
            holding[i] = holding[i] + addition
            surplus = surplus - addition
    return np.array([most] + holding)


def ragged_sizes(key, amount, total, bound, skew):
    if amount == 2:
        one = jax.random.randint(key, (), max(1, total - bound), min(bound, total - 1) + 1)
        return jnp.stack([one, total - one])
    lengths = jnp.asarray(profile(amount, total, bound, skew), jnp.int32)
    pairs = (amount - 1) // 2
    source_of, taker = lengths[1:1 + 2 * pairs:2], lengths[2:2 + 2 * pairs:2]
    room = jnp.minimum(source_of - 1, bound - taker)
    shifted = jax.random.randint(jax.random.fold_in(key, 1), (pairs,), 0, 1 << 20) % (room + 1)
    lengths = lengths.at[1:1 + 2 * pairs:2].set(source_of - shifted).at[2:2 + 2 * pairs:2].set(taker + shifted)
    return lengths[jax.random.permutation(jax.random.fold_in(key, 2), amount)]


def routed_block(stream_key, own, number, rows, number_of, top, most, skew):
    ranking = jax.random.permutation(stream_key, number_of)
    crowded, usual = load_shares(number_of, rows * top, most, skew, True), load_shares(number_of, rows * top, most, skew, False)
    places = jnp.arange(number_of)

    def named(lengths, rotation):
        used = int((lengths > 0).sum())
        fixed = max(1, used // 4)
        shifted = fixed + (places - fixed + rotation * (used - fixed)) % max(1, number_of - fixed)
        return jnp.zeros((number_of,), jnp.int32).at[ranking[jnp.where(places < fixed, places, shifted)]].set(jnp.asarray(lengths, jnp.int32))

    lengths = jnp.where(number % 4 == 0, named(crowded, number // 4), named(usual, number - number // 4 - 1))
    mixed = jax.random.permutation(jax.random.fold_in(own, 3), number_of)
    giver, taker = mixed[0:number_of // 2 * 2:2], mixed[1:number_of // 2 * 2:2]
    room = jnp.minimum(lengths[giver] - 1, most - lengths[taker]) // 2
    room = jnp.where((giver == ranking[0]) | (taker == ranking[0]) | (lengths[taker] == 0), 0, jnp.maximum(room, 0))
    shifted = jax.random.randint(jax.random.fold_in(own, 4), (number_of // 2,), 0, 1 << 20) % (room + 1)
    lengths = lengths.at[giver].add(-shifted).at[taker].add(shifted)
    items = jnp.searchsorted(jnp.cumsum(lengths), jnp.arange(rows * top), side="right").astype(jnp.int32)
    grid = items.reshape(top, rows).T
    grid = grid[jax.random.permutation(jax.random.fold_in(own, 1), rows)]
    rotation = jax.random.randint(jax.random.fold_in(own, 2), (rows, 1), 0, top)
    return jnp.take_along_axis(grid, (jnp.arange(top)[None, :] + rotation) % top, axis=1)


def load_shares(number_of, total, reach, slope, full):
    loads = [(1 << 20) // math.isqrt(rank ** slope) + 1 for rank in range(1, number_of + 1)]
    largest = reach if full else min(reach, max(-(-total // number_of), total * loads[0] // sum(loads)))
    least = 1 if total - largest >= number_of - 1 else 0
    holding, rest = [largest] + [least] * (number_of - 1), total - largest - least * (number_of - 1)
    while rest > 0:
        movable = [i for i in range(1, number_of) if holding[i] < largest] or [i for i in range(1, number_of) if holding[i] < reach]
        mass, remaining = sum([loads[i] for i in movable]), rest
        for i in movable:
            extra = min(reach - holding[i], max(1, remaining * loads[i] // mass), rest)
            holding[i] = holding[i] + extra
            rest = rest - extra
    return np.array(holding)


def normal_values(key, shape, width, bound, shards=(), kind=jnp.bfloat16):
    level = shard_levels(key, shape, shards, -0.22, 0.18) if shards else 1.0
    array = jax.random.normal(key, shape, jnp.float32) * width * level
    return jnp.minimum(jnp.maximum(array, -bound), bound).astype(kind)


def setup_inputs(seed: int = 0, part: int = 0) -> dict:
    keys = jax.random.split(jax.random.key(seed), 9)
    part_splits = jax.random.split(jax.random.fold_in(keys[8], part), 9)
    tokens = normal_values(part_splits[0], (TOKENS, D), 1.0, 6.0, ((0, 8),))
    norm_gain = jnp.clip(1.0 + 0.18 * jax.random.normal(keys[1], (D,), jnp.float32), 0.1, 1.9)
    expert_ids_keys = jax.random.split(jax.random.fold_in(part_splits[2], 1), TOKENS // TOK_DEV)
    expert_ids_turns = jax.random.permutation(jax.random.fold_in(part_splits[2], 3), TOKENS // TOK_DEV)
    expert_ids = jax.vmap(lambda own, number: routed_block(jax.random.fold_in(part_splits[2], 2), own, number, TOK_DEV, EXPERTS, TOPK, CAP, 2))(expert_ids_keys, expert_ids_turns).reshape((TOKENS, TOPK))
    gate_vals = jnp.clip(jnp.exp(math.log(4.0) - 2.7725887 * jax.random.uniform(part_splits[3], (TOKENS, TOPK), jnp.float32) ** shard_levels(part_splits[3], (TOKENS, TOPK), ((0, 8),), -0.2, 0.2)), 0.25, 4.0)
    live_counts = ragged_sizes(part_splits[4], N_EP, N_EP * TOK_DEV * 7 // 8, TOK_DEV, 1).astype(jnp.int32)
    w_gate = normal_values(keys[5], (D, FLIGHT * H), D ** -0.5, 0.125, ((1, 8),))
    w_up = normal_values(keys[6], (D, FLIGHT * H), D ** -0.5, 0.125, ((1, 8),))
    w_down = normal_values(keys[7], (FLIGHT * H, D), H ** -0.5, 0.15625, ((0, 8),))
    return {"tokens": tokens, "norm_gain": norm_gain, "expert_ids": expert_ids, "gate_vals": gate_vals, "live_counts": live_counts, "w_gate": w_gate, "w_up": w_up, "w_down": w_down}


def reference(tokens, norm_gain, expert_ids, gate_vals, live_counts, w_gate, w_up, w_down):
    values = tokens.astype(jnp.float32)
    mean_sq = lax.optimization_barrier(jnp.mean(values * values, axis=-1, keepdims=True))
    normed = (values * lax.rsqrt(mean_sq + 1e-06) * norm_gain).astype(jnp.bfloat16)
    position = jnp.arange(TOKENS, dtype=jnp.int32)
    live = position % TOK_DEV < live_counts[position // TOK_DEV]
    rows_max = N_EP * CAP
    slice_width = H // SLICES

    def one_expert(accum, expert):
        match = (expert_ids == expert) & live[:, None]
        weight = lax.optimization_barrier(jnp.sum(jnp.where(match, gate_vals, jnp.zeros_like(gate_vals)), axis=1))
        chosen = jnp.any(match, axis=1)
        index = jnp.nonzero(chosen, size=rows_max, fill_value=0)[0].astype(jnp.int32)
        valid = jnp.arange(rows_max, dtype=jnp.int32) < jnp.sum(chosen.astype(jnp.int32))
        picked = normed[index]
        gate_cols = lax.dynamic_slice_in_dim(w_gate, expert * H, H, 1)
        up_cols = lax.dynamic_slice_in_dim(w_up, expert * H, H, 1)
        down_rows = lax.dynamic_slice_in_dim(w_down, expert * H, H, 0)
        gate_act = jnp.dot(picked, gate_cols, preferred_element_type=jnp.float32)
        up_act = jnp.dot(picked, up_cols, preferred_element_type=jnp.float32)
        hidden = (jax.nn.silu(gate_act) * up_act).astype(jnp.bfloat16)
        partial_out = jnp.einsum('nsh,shd->nsd', hidden.reshape(rows_max, SLICES, slice_width).astype(jnp.float32), down_rows.reshape(SLICES, slice_width, D).astype(jnp.float32))
        level = lax.optimization_barrier(partial_out.astype(jnp.bfloat16))
        for _ in range(SLICES.bit_length() - 1):
            added = level[:, 0::2].astype(jnp.float32) + level[:, 1::2].astype(jnp.float32)
            level = lax.optimization_barrier(added.astype(jnp.bfloat16))
        expert_out = level[:, 0].astype(jnp.float32)
        scale = jnp.where(valid, weight[index], jnp.zeros_like(weight[index]))
        accum = accum.at[index].add(scale[:, None] * expert_out)
        return (accum, None)
    start = jnp.zeros((TOKENS, D), jnp.float32)
    total, _ = lax.scan(one_expert, start, jnp.arange(FLIGHT, dtype=jnp.int32))
    return total.astype(jnp.bfloat16)
```

```python
import functools

import jax
import jax.numpy as jnp
from jax import lax
from jax.experimental import pallas as pl
from jax.experimental.pallas import tpu as pltpu
from jax.sharding import PartitionSpec as P

SLICES = 8
CAP = 16
VMEM_LIMIT = 40 * 1024 * 1024


def pick_kernel(live_ref, ids_ref, gate_ref, tokens_ref, gain_ref, rows_ref, table_ref):
    slots, tok_rows = table_ref.shape
    slot = lax.broadcasted_iota(jnp.int32, (slots, tok_rows), 0)
    token = lax.broadcasted_iota(jnp.int32, (slots, tok_rows), 1)
    expert, place = slot // CAP, slot % CAP
    live = token < live_ref[0]
    chosen = jnp.zeros((slots, tok_rows), jnp.float32)
    weight = jnp.zeros((slots, tok_rows), jnp.float32)
    for k in range(ids_ref.shape[0]):
        hit = (ids_ref[k : k + 1, :] == expert) & live
        chosen = jnp.where(hit, 1.0, chosen)
        weight = jnp.where(hit, gate_ref[k : k + 1, :], weight)
    before = lax.broadcasted_iota(jnp.int32, (tok_rows, tok_rows), 0)
    after = lax.broadcasted_iota(jnp.int32, (tok_rows, tok_rows), 1)
    earlier = jnp.where(before < after, 1.0, 0.0).astype(jnp.bfloat16)
    rank = jnp.dot(chosen.astype(jnp.bfloat16), earlier, preferred_element_type=jnp.float32)
    pick = jnp.where((chosen > 0.0) & (rank.astype(jnp.int32) == place), 1.0, 0.0)
    table_ref[...] = pick * weight
    values = jnp.dot(pick.astype(jnp.bfloat16), tokens_ref[...], preferred_element_type=jnp.float32)
    mean_sq = jnp.mean(values * values, axis=-1, keepdims=True)
    rows_ref[...] = (values * lax.rsqrt(mean_sq + 1e-06) * gain_ref[...]).astype(jnp.bfloat16)


def pick_rows(slots, live_counts, ids, gate_vals, tokens, gain):
    vmem = pl.BlockSpec(memory_space=pltpu.VMEM)
    return pl.pallas_call(
        pick_kernel,
        out_shape=(
            jax.ShapeDtypeStruct((slots, tokens.shape[1]), jnp.bfloat16),
            jax.ShapeDtypeStruct((slots, tokens.shape[0]), jnp.float32),
        ),
        in_specs=[pl.BlockSpec(memory_space=pltpu.SMEM), vmem, vmem, vmem, vmem],
        out_specs=(vmem, vmem),
        compiler_params=pltpu.CompilerParams(vmem_limit_bytes=VMEM_LIMIT),
        name="pick_rows",
    )(live_counts, ids, gate_vals, tokens, gain)


def expert_kernel(rows_ref, gate_ref, up_ref, down_ref, out_ref):
    dims = (((1,), (1,)), ((), ()))
    rows = rows_ref[...]
    gate_act = lax.dot_general(rows, gate_ref[...], dims, preferred_element_type=jnp.float32)
    up_act = lax.dot_general(rows, up_ref[...], dims, preferred_element_type=jnp.float32)
    hidden = (jax.nn.silu(gate_act) * up_act).astype(jnp.bfloat16)
    out_ref[...] = jnp.dot(hidden, down_ref[...], preferred_element_type=jnp.float32).astype(
        jnp.bfloat16
    )


def expert_slice(rows, gate_rows, up_rows, down_rows):
    count, features = rows.shape
    block = min(count, 128)
    whole = pl.BlockSpec(gate_rows.shape, lambda i: (0, 0))
    return pl.pallas_call(
        expert_kernel,
        grid=(count // block,),
        out_shape=jax.ShapeDtypeStruct((count, features), jnp.bfloat16),
        in_specs=[pl.BlockSpec((block, features), lambda i: (i, 0)), whole, whole, whole],
        out_specs=pl.BlockSpec((block, features), lambda i: (i, 0)),
        compiler_params=pltpu.CompilerParams(vmem_limit_bytes=VMEM_LIMIT),
        name="expert_slice",
    )(rows, gate_rows, up_rows, down_rows)


def combine_kernel(table_ref, kept_ref, came_ref, out_ref):
    dims = (((0,), (0,)), ((), ()))
    summed = (kept_ref[...].astype(jnp.float32) + came_ref[...].astype(jnp.float32)).astype(
        jnp.bfloat16
    )
    table = table_ref[...]
    result = jnp.zeros(out_ref.shape, jnp.float32)
    for _ in range(3):
        piece = table.astype(jnp.bfloat16)
        result = result + lax.dot_general(piece, summed, dims, preferred_element_type=jnp.float32)
        table = table - piece.astype(jnp.float32)
    out_ref[...] = result.astype(jnp.bfloat16)


def combine(table, kept, came):
    vmem = pl.BlockSpec(memory_space=pltpu.VMEM)
    return pl.pallas_call(
        combine_kernel,
        out_shape=jax.ShapeDtypeStruct((table.shape[1], kept.shape[1]), jnp.bfloat16),
        in_specs=[vmem, vmem, vmem],
        out_specs=vmem,
        compiler_params=pltpu.CompilerParams(vmem_limit_bytes=VMEM_LIMIT),
        name="combine",
    )(table, kept, came)


def across_groups(flight, blocks):
    if flight == 1:
        return blocks
    groups = [[g * SLICES + m for g in range(flight)] for m in range(SLICES)]
    return lax.all_to_all(
        blocks, "ep", split_axis=0, concat_axis=0, axis_index_groups=groups, tiled=True
    )


def swap(devices, distance, block):
    return lax.ppermute(block, "ep", [(i, i ^ distance) for i in range(devices)])


def add_level(kept, came):
    return (kept.astype(jnp.float32) + came.astype(jnp.float32)).astype(jnp.bfloat16)


def on_device(tokens, norm_gain, expert_ids, gate_vals, live_counts, w_gate, w_up, w_down):
    features = tokens.shape[1]
    devices = lax.axis_size("ep")
    flight = devices // SLICES
    slots = flight * CAP
    rows, table = pick_rows(
        slots, live_counts, expert_ids.T, gate_vals.T, tokens, norm_gain.reshape(1, features)
    )
    own = across_groups(flight, rows)
    groups = [[g * SLICES + m for m in range(SLICES)] for g in range(flight)]
    arrived = lax.all_gather(own, "ep", axis_index_groups=groups, tiled=True)
    partial_out = expert_slice(arrived, w_gate.T, w_up.T, w_down)
    me = lax.axis_index("ep")
    level = partial_out.reshape(SLICES // 2, 2, slots, features)
    for bit in range(3):
        mine = (me >> bit) & 1
        kept = lax.dynamic_index_in_dim(level, mine, 1, keepdims=False)
        sent = lax.dynamic_index_in_dim(level, 1 - mine, 1, keepdims=False)
        came = swap(devices, 1 << bit, sent)
        if bit < 2:
            level = add_level(kept, came).reshape(-1, 2, slots, features)
    kept, came = (across_groups(flight, part.reshape(slots, features)) for part in (kept, came))
    return combine(table, kept, came)


def solution(mesh):
    return jax.shard_map(
        on_device,
        mesh=mesh,
        in_specs=(
            P(("sp", "ep"), None),
            P(),
            P(("sp", "ep"), None),
            P(("sp", "ep"), None),
            P(("sp", "ep")),
            P(None, "ep"),
            P(None, "ep"),
            P("ep", None),
        ),
        out_specs=P(("sp", "ep"), None),
        check_vma=False,
    )
```

```python
import functools

import jax
import jax.numpy as jnp
from jax import lax
from jax.experimental import pallas as pl
from jax.experimental.pallas import tpu as pltpu
from jax.sharding import PartitionSpec as P

SLICES = 8
CAP = 16
VMEM_LIMIT = 40 * 1024 * 1024


def pick_kernel(
    live_ref, ids_hbm, gate_hbm, tokens_hbm, gain_hbm, rows_ref, table_ref, ids_ref, gate_ref, tokens_ref, gain_ref, sems
):
    copies = [
        pltpu.make_async_copy(source, target, sems.at[i])
        for i, (source, target) in enumerate(
            ((ids_hbm, ids_ref), (tokens_hbm, tokens_ref), (gate_hbm, gate_ref), (gain_hbm, gain_ref))
        )
    ]
    for copy in copies:
        copy.start()
    slots, tok_rows = table_ref.shape
    slot = lax.broadcasted_iota(jnp.int32, (slots, tok_rows), 0)
    token = lax.broadcasted_iota(jnp.int32, (slots, tok_rows), 1)
    expert, place = slot // CAP, slot % CAP
    live = token < live_ref[0]
    before = lax.broadcasted_iota(jnp.int32, (tok_rows, tok_rows), 0)
    after = lax.broadcasted_iota(jnp.int32, (tok_rows, tok_rows), 1)
    earlier = jnp.where(before < after, 1.0, 0.0).astype(jnp.bfloat16)
    copies[0].wait()
    hits = [(ids_ref[k : k + 1, :] == expert) & live for k in range(ids_ref.shape[0])]
    chosen = jnp.where(functools.reduce(jnp.logical_or, hits), 1.0, 0.0)
    rank = jnp.dot(chosen.astype(jnp.bfloat16), earlier, preferred_element_type=jnp.float32)
    pick = jnp.where((chosen > 0.0) & (rank.astype(jnp.int32) == place), 1.0, 0.0)
    copies[1].wait()
    values = jnp.dot(pick.astype(jnp.bfloat16), tokens_ref[...], preferred_element_type=jnp.float32)
    mean_sq = jnp.mean(values * values, axis=-1, keepdims=True)
    copies[2].wait()
    copies[3].wait()
    rows_ref[...] = (values * lax.rsqrt(mean_sq + 1e-06) * gain_ref[...]).astype(jnp.bfloat16)
    weight = jnp.zeros((slots, tok_rows), jnp.float32)
    for k, hit in enumerate(hits):
        weight = jnp.where(hit, gate_ref[k : k + 1, :], weight)
    table_ref[...] = pick * weight


def pick_rows(slots, live_counts, ids, gate_vals, tokens, gain):
    vmem = pl.BlockSpec(memory_space=pltpu.VMEM)
    hbm = pl.BlockSpec(memory_space=pltpu.HBM)
    return pl.pallas_call(
        pick_kernel,
        out_shape=(
            jax.ShapeDtypeStruct((slots, tokens.shape[1]), jnp.bfloat16),
            jax.ShapeDtypeStruct((slots, tokens.shape[0]), jnp.float32),
        ),
        in_specs=[pl.BlockSpec(memory_space=pltpu.SMEM), hbm, hbm, hbm, hbm],
        out_specs=(vmem, vmem),
        scratch_shapes=[
            pltpu.VMEM(ids.shape, ids.dtype),
            pltpu.VMEM(gate_vals.shape, gate_vals.dtype),
            pltpu.VMEM(tokens.shape, tokens.dtype),
            pltpu.VMEM(gain.shape, gain.dtype),
            pltpu.SemaphoreType.DMA((4,)),
        ],
        compiler_params=pltpu.CompilerParams(vmem_limit_bytes=VMEM_LIMIT),
        name="pick_rows",
    )(live_counts, ids, gate_vals, tokens, gain)


def expert_kernel(*refs):
    count = (len(refs) - 3) // 2
    gate_ref, up_ref, down_ref = refs[count : count + 3]
    dims = (((1,), (1,)), ((), ()))
    size = refs[0].shape[0]
    together = max(1, 128 // size)
    for first in range(0, count, together):
        last = min(count, first + together)
        rows = jnp.concatenate([ref[...] for ref in refs[first:last]], axis=0)
        gate_act = lax.dot_general(rows, gate_ref[...], dims, preferred_element_type=jnp.float32)
        up_act = lax.dot_general(rows, up_ref[...], dims, preferred_element_type=jnp.float32)
        hidden = (jax.nn.silu(gate_act) * up_act).astype(jnp.bfloat16)
        partial_out = jnp.dot(hidden, down_ref[...], preferred_element_type=jnp.float32)
        partial_out = partial_out.astype(jnp.bfloat16)
        for i in range(first, last):
            at = (i - first) * size
            refs[count + 3 + i][...] = partial_out[at : at + size]


def expert_slice(blocks, gate_rows, up_rows, down_rows):
    vmem = pl.BlockSpec(memory_space=pltpu.VMEM)
    count = len(blocks)
    return pl.pallas_call(
        expert_kernel,
        out_shape=[jax.ShapeDtypeStruct(block.shape, jnp.bfloat16) for block in blocks],
        in_specs=[vmem] * (count + 3),
        out_specs=[vmem] * count,
        compiler_params=pltpu.CompilerParams(vmem_limit_bytes=VMEM_LIMIT),
        name="expert_slice",
    )(*blocks, gate_rows, up_rows, down_rows)


def add_level(kept, came):
    return (kept.astype(jnp.float32) + came.astype(jnp.float32)).astype(jnp.bfloat16)


def add_levels(parts):
    while len(parts) > 1:
        parts = [add_level(*pair) for pair in zip(parts[::2], parts[1::2])]
    return parts[0]


def combine_kernel(table_ref, *refs):
    *parts, out_hbm, out_ref, sems = refs
    table = table_ref[...]
    pieces = []
    for _ in range(3):
        pieces.append(table.astype(jnp.bfloat16))
        table = table - pieces[-1].astype(jnp.float32)
    pieces = jnp.concatenate(pieces, axis=0)
    features = out_ref.shape[1]
    width = features // 4
    copies = []
    for i in range(4):
        columns = pl.ds(i * width, width)
        summed = add_levels([part[:, columns] for part in parts])
        out_ref[:, columns] = lax.dot_general(
            pieces,
            jnp.concatenate([summed] * 3, axis=0),
            (((0,), (0,)), ((), ())),
            preferred_element_type=jnp.float32,
        ).astype(jnp.bfloat16)
        copies.append(
            pltpu.make_async_copy(out_ref.at[:, columns], out_hbm.at[:, columns], sems.at[i])
        )
        copies[-1].start()
    for copy in copies:
        copy.wait()


def combine(table, parts):
    vmem = pl.BlockSpec(memory_space=pltpu.VMEM)
    shape = (table.shape[1], parts[0].shape[1])
    return pl.pallas_call(
        combine_kernel,
        out_shape=jax.ShapeDtypeStruct(shape, jnp.bfloat16),
        in_specs=[vmem] * (1 + len(parts)),
        out_specs=pl.BlockSpec(memory_space=pltpu.HBM),
        scratch_shapes=[pltpu.VMEM(shape, jnp.bfloat16), pltpu.SemaphoreType.DMA((4,))],
        compiler_params=pltpu.CompilerParams(vmem_limit_bytes=VMEM_LIMIT),
        name="combine",
    )(table, *parts)


def across_groups(flight, blocks):
    if flight == 1:
        return blocks
    groups = [[g * SLICES + m for g in range(flight)] for m in range(SLICES)]
    return lax.all_to_all(
        blocks, "ep", split_axis=0, concat_axis=0, axis_index_groups=groups, tiled=True
    )


def swap(devices, distance, block):
    return lax.ppermute(block, "ep", [(i, i ^ distance) for i in range(devices)])


def on_device(tokens, norm_gain, expert_ids, gate_vals, live_counts, w_gate, w_up, w_down):
    features = tokens.shape[1]
    devices = lax.axis_size("ep")
    flight = devices // SLICES
    slots = flight * CAP
    rows, table = pick_rows(
        slots, live_counts, expert_ids.T, gate_vals.T, tokens, norm_gain.reshape(1, features)
    )
    own = across_groups(flight, rows)
    blocks = {0: own}
    for j in (6, 4, 2, 1):
        blocks[j] = swap(devices, j, own)
    for j in (2, 4, 6):
        blocks[j + 1] = swap(devices, 1, blocks[j])
    partial_out = expert_slice(
        [blocks[j] for j in range(SLICES)], w_gate.T, w_up.T, w_down
    )
    level = {}
    for j in (6, 4, 2, 0):
        level[j] = add_level(partial_out[j], swap(devices, 1, partial_out[j + 1]))
    parts = [level[0]] + [swap(devices, j, level[j]) for j in (2, 4, 6)]
    if flight > 1:
        parts = [across_groups(flight, add_levels(parts))]
    return combine(table, parts)


def solution(mesh):
    return jax.shard_map(
        on_device,
        mesh=mesh,
        in_specs=(
            P(("sp", "ep"), None),
            P(),
            P(("sp", "ep"), None),
            P(("sp", "ep"), None),
            P(("sp", "ep")),
            P(None, "ep"),
            P(None, "ep"),
            P("ep", None),
        ),
        out_specs=P(("sp", "ep"), None),
        check_vma=False,
    )
```

```python
import functools

import jax
import jax.numpy as jnp
from jax import lax
from jax.experimental import pallas as pl
from jax.experimental.pallas import tpu as pltpu
from jax.sharding import PartitionSpec as P

SLICES = 8
CAP = 16
VMEM_LIMIT = 40 * 1024 * 1024


def in_hbm(array):
    return pltpu.with_memory_space_constraint(array, pltpu.HBM)


def pick_kernel(
    live_ref, ids_hbm, gate_hbm, tokens_hbm, gain_hbm, rows_ref, table_ref, ids_ref, gate_ref, tokens_ref, gain_ref, sems
):
    copies = [
        pltpu.make_async_copy(source, target, sems.at[i])
        for i, (source, target) in enumerate(
            ((ids_hbm, ids_ref), (tokens_hbm, tokens_ref), (gate_hbm, gate_ref), (gain_hbm, gain_ref))
        )
    ]
    for copy in copies:
        copy.start()
    slots, tok_rows = table_ref.shape
    slot = lax.broadcasted_iota(jnp.int32, (slots, tok_rows), 0)
    token = lax.broadcasted_iota(jnp.int32, (slots, tok_rows), 1)
    expert, place = slot // CAP, slot % CAP
    live = token < live_ref[0]
    before = lax.broadcasted_iota(jnp.int32, (tok_rows, tok_rows), 0)
    after = lax.broadcasted_iota(jnp.int32, (tok_rows, tok_rows), 1)
    earlier = jnp.where(before < after, 1.0, 0.0).astype(jnp.bfloat16)
    copies[0].wait()
    hits = [(ids_ref[k : k + 1, :] == expert) & live for k in range(ids_ref.shape[0])]
    chosen = jnp.where(functools.reduce(jnp.logical_or, hits), 1.0, 0.0)
    rank = jnp.dot(chosen.astype(jnp.bfloat16), earlier, preferred_element_type=jnp.float32)
    pick = jnp.where((chosen > 0.0) & (rank.astype(jnp.int32) == place), 1.0, 0.0)
    copies[1].wait()
    values = jnp.dot(pick.astype(jnp.bfloat16), tokens_ref[...], preferred_element_type=jnp.float32)
    mean_sq = jnp.mean(values * values, axis=-1, keepdims=True)
    copies[2].wait()
    copies[3].wait()
    rows_ref[...] = (values * lax.rsqrt(mean_sq + 1e-06) * gain_ref[...]).astype(jnp.bfloat16)
    weight = jnp.zeros((slots, tok_rows), jnp.float32)
    for k, hit in enumerate(hits):
        weight = jnp.where(hit, gate_ref[k : k + 1, :], weight)
    table_ref[...] = pick * weight


def pick_rows(slots, live_counts, ids, gate_vals, tokens, gain):
    vmem = pl.BlockSpec(memory_space=pltpu.VMEM)
    hbm = pl.BlockSpec(memory_space=pltpu.HBM)
    return pl.pallas_call(
        pick_kernel,
        out_shape=(
            jax.ShapeDtypeStruct((slots, tokens.shape[1]), jnp.bfloat16),
            jax.ShapeDtypeStruct((slots, tokens.shape[0]), jnp.float32),
        ),
        in_specs=[pl.BlockSpec(memory_space=pltpu.SMEM), hbm, hbm, hbm, hbm],
        out_specs=(vmem, vmem),
        scratch_shapes=[
            pltpu.VMEM(ids.shape, ids.dtype),
            pltpu.VMEM(gate_vals.shape, gate_vals.dtype),
            pltpu.VMEM(tokens.shape, tokens.dtype),
            pltpu.VMEM(gain.shape, gain.dtype),
            pltpu.SemaphoreType.DMA((4,)),
        ],
        compiler_params=pltpu.CompilerParams(vmem_limit_bytes=VMEM_LIMIT),
        name="pick_rows",
    )(live_counts, *(in_hbm(array) for array in (ids, gate_vals, tokens, gain)))


def expert_rows(rows, gate_ref, up_ref, down_ref):
    dims = (((1,), (1,)), ((), ()))
    gate_act = lax.dot_general(rows, gate_ref[...], dims, preferred_element_type=jnp.float32)
    up_act = lax.dot_general(rows, up_ref[...], dims, preferred_element_type=jnp.float32)
    hidden = (jax.nn.silu(gate_act) * up_act).astype(jnp.bfloat16)
    partial_out = jnp.dot(hidden, down_ref[...], preferred_element_type=jnp.float32)
    return partial_out.astype(jnp.bfloat16)


def expert_cost(rows, weights):
    size = sum(weight.size for weight in weights)
    return pl.CostEstimate(flops=2 * rows * size, bytes_accessed=2 * size, transcendentals=0)


def first_kernel(rows_ref, gate_hbm, up_hbm, down_hbm, out_ref, gate_ref, up_ref, down_ref, sems):
    copies = [
        pltpu.make_async_copy(source, target, sems.at[i])
        for i, (source, target) in enumerate(
            ((gate_hbm, gate_ref), (up_hbm, up_ref), (down_hbm, down_ref))
        )
    ]
    for copy in copies:
        copy.start()
    for copy in copies:
        copy.wait()
    out_ref[...] = expert_rows(rows_ref[...], gate_ref, up_ref, down_ref)


def first_slice(rows, weights):
    vmem = pl.BlockSpec(memory_space=pltpu.VMEM)
    hbm = pl.BlockSpec(memory_space=pltpu.HBM)
    return pl.pallas_call(
        first_kernel,
        out_shape=[jax.ShapeDtypeStruct(rows.shape, jnp.bfloat16)]
        + [jax.ShapeDtypeStruct(weight.shape, weight.dtype) for weight in weights],
        in_specs=[vmem, hbm, hbm, hbm],
        out_specs=[vmem] * 4,
        scratch_shapes=[pltpu.SemaphoreType.DMA((3,))],
        compiler_params=pltpu.CompilerParams(vmem_limit_bytes=VMEM_LIMIT),
        cost_estimate=expert_cost(rows.shape[0], weights),
        name="first_slice",
    )(rows, *(in_hbm(weight) for weight in weights))


def expert_kernel(*refs):
    count = (len(refs) - 3) // 2
    weights = refs[count : count + 3]
    size = refs[0].shape[0]
    together = max(1, 128 // size)
    for first in range(0, count, together):
        last = min(count, first + together)
        rows = jnp.concatenate([ref[...] for ref in refs[first:last]], axis=0)
        partial_out = expert_rows(rows, *weights)
        for i in range(first, last):
            at = (i - first) * size
            refs[count + 3 + i][...] = partial_out[at : at + size]


def expert_slice(blocks, weights):
    vmem = pl.BlockSpec(memory_space=pltpu.VMEM)
    count = len(blocks)
    return pl.pallas_call(
        expert_kernel,
        out_shape=[jax.ShapeDtypeStruct(block.shape, jnp.bfloat16) for block in blocks],
        in_specs=[vmem] * (count + 3),
        out_specs=[vmem] * count,
        compiler_params=pltpu.CompilerParams(vmem_limit_bytes=VMEM_LIMIT),
        cost_estimate=expert_cost(count * blocks[0].shape[0], weights),
        name="expert_slice",
    )(*blocks, *weights)


def add_level(kept, came):
    return (kept.astype(jnp.float32) + came.astype(jnp.float32)).astype(jnp.bfloat16)


def add_levels(parts):
    while len(parts) > 1:
        parts = [add_level(*pair) for pair in zip(parts[::2], parts[1::2])]
    return parts[0]


def combine_kernel(table_ref, *refs):
    *parts, out_hbm, out_ref, sems = refs
    table = table_ref[...]
    pieces = []
    for _ in range(3):
        pieces.append(table.astype(jnp.bfloat16))
        table = table - pieces[-1].astype(jnp.float32)
    pieces = jnp.concatenate(pieces, axis=0)
    features = out_ref.shape[1]
    width = features // 4
    copies = []
    for i in range(4):
        columns = pl.ds(i * width, width)
        summed = add_levels([part[:, columns] for part in parts])
        out_ref[:, columns] = lax.dot_general(
            pieces,
            jnp.concatenate([summed] * 3, axis=0),
            (((0,), (0,)), ((), ())),
            preferred_element_type=jnp.float32,
        ).astype(jnp.bfloat16)
        copies.append(
            pltpu.make_async_copy(out_ref.at[:, columns], out_hbm.at[:, columns], sems.at[i])
        )
        copies[-1].start()
    for copy in copies:
        copy.wait()


def combine(table, parts):
    vmem = pl.BlockSpec(memory_space=pltpu.VMEM)
    shape = (table.shape[1], parts[0].shape[1])
    return pl.pallas_call(
        combine_kernel,
        out_shape=jax.ShapeDtypeStruct(shape, jnp.bfloat16),
        in_specs=[vmem] * (1 + len(parts)),
        out_specs=pl.BlockSpec(memory_space=pltpu.HBM),
        scratch_shapes=[pltpu.VMEM(shape, jnp.bfloat16), pltpu.SemaphoreType.DMA((4,))],
        compiler_params=pltpu.CompilerParams(vmem_limit_bytes=VMEM_LIMIT),
        name="combine",
    )(table, *parts)


def across_groups(flight, blocks):
    if flight == 1:
        return blocks
    groups = [[g * SLICES + m for g in range(flight)] for m in range(SLICES)]
    return lax.all_to_all(
        blocks, "ep", split_axis=0, concat_axis=0, axis_index_groups=groups, tiled=True
    )


def swap(devices, distance, block):
    return lax.ppermute(block, "ep", [(i, i ^ distance) for i in range(devices)])


def on_device(tokens, norm_gain, expert_ids, gate_vals, live_counts, w_gate, w_up, w_down):
    features = tokens.shape[1]
    devices = lax.axis_size("ep")
    flight = devices // SLICES
    slots = flight * CAP
    rows, table = pick_rows(
        slots, live_counts, expert_ids.T, gate_vals.T, tokens, norm_gain.reshape(1, features)
    )
    own = across_groups(flight, rows)
    blocks = {0: own}
    for j in (6, 4, 2, 1):
        blocks[j] = swap(devices, j, own)
    for j in (2, 4, 6):
        blocks[j + 1] = swap(devices, 1, blocks[j])
    partial_out = {}
    partial_out[0], *weights = first_slice(own, (w_gate.T, w_up.T, w_down))
    for group in ((1, 2, 4, 6), (3, 5, 7)):
        outs = expert_slice([blocks[j] for j in group], weights)
        partial_out.update(zip(group, outs))
    level = {}
    for j in (6, 4, 2, 0):
        level[j] = add_level(partial_out[j], swap(devices, 1, partial_out[j + 1]))
    parts = [level[0]] + [swap(devices, j, level[j]) for j in (2, 4, 6)]
    if flight > 1:
        parts = [across_groups(flight, add_levels(parts))]
    return combine(table, parts)


def solution(mesh):
    return jax.shard_map(
        on_device,
        mesh=mesh,
        in_specs=(
            P(("sp", "ep"), None),
            P(),
            P(("sp", "ep"), None),
            P(("sp", "ep"), None),
            P(("sp", "ep")),
            P(None, "ep"),
            P(None, "ep"),
            P("ep", None),
        ),
        out_specs=P(("sp", "ep"), None),
        check_vma=False,
    )
```

```python
import functools

import jax
import jax.numpy as jnp
from jax import lax
from jax.experimental import pallas as pl
from jax.experimental.pallas import tpu as pltpu
from jax.sharding import PartitionSpec as P

SLICES = 8
CAP = 16
VMEM_LIMIT = 40 * 1024 * 1024
WEIGHT_CHUNKS = 4
TOKEN_CHUNKS = 4


def in_hbm(array):
    return pltpu.with_memory_space_constraint(array, pltpu.HBM)


def pick_kernel(
    live_ref, ids_hbm, gate_hbm, tokens_hbm, gain_hbm, rows_ref, table_ref, ids_ref, gate_ref, tokens_ref, gain_ref, sems
):
    ids_copy, gate_copy, gain_copy = (
        pltpu.make_async_copy(source, target, sems.at[TOKEN_CHUNKS + i])
        for i, (source, target) in enumerate(
            ((ids_hbm, ids_ref), (gate_hbm, gate_ref), (gain_hbm, gain_ref))
        )
    )
    token_copies = list(chunk_copies(tokens_hbm, tokens_ref, TOKEN_CHUNKS, sems))
    for copy in (ids_copy, *token_copies, gain_copy, gate_copy):
        copy.start()
    slots, tok_rows = table_ref.shape
    slot = lax.broadcasted_iota(jnp.int32, (slots, tok_rows), 0)
    token = lax.broadcasted_iota(jnp.int32, (slots, tok_rows), 1)
    expert, place = slot // CAP, slot % CAP
    live = token < live_ref[0]
    before = lax.broadcasted_iota(jnp.int32, (tok_rows, tok_rows), 0)
    after = lax.broadcasted_iota(jnp.int32, (tok_rows, tok_rows), 1)
    earlier = jnp.where(before < after, 1.0, 0.0).astype(jnp.bfloat16)
    ids_copy.wait()
    hits = [(ids_ref[k : k + 1, :] == expert) & live for k in range(ids_ref.shape[0])]
    chosen = jnp.where(functools.reduce(jnp.logical_or, hits), 1.0, 0.0)
    rank = jnp.dot(chosen.astype(jnp.bfloat16), earlier, preferred_element_type=jnp.float32)
    pick = jnp.where((chosen > 0.0) & (rank.astype(jnp.int32) == place), 1.0, 0.0)
    for copy in token_copies:
        copy.wait()
    values = jnp.dot(pick.astype(jnp.bfloat16), tokens_ref[...], preferred_element_type=jnp.float32)
    mean_sq = jnp.mean(values * values, axis=-1, keepdims=True)
    gain_copy.wait()
    rows_ref[...] = (values * lax.rsqrt(mean_sq + 1e-06) * gain_ref[...]).astype(jnp.bfloat16)
    gate_copy.wait()
    weight = jnp.zeros((slots, tok_rows), jnp.float32)
    for k, hit in enumerate(hits):
        weight = jnp.where(hit, gate_ref[k : k + 1, :], weight)
    table_ref[...] = pick * weight


def pick_rows(slots, live_counts, ids, gate_vals, tokens, gain):
    vmem = pl.BlockSpec(memory_space=pltpu.VMEM)
    hbm = pl.BlockSpec(memory_space=pltpu.HBM)
    return pl.pallas_call(
        pick_kernel,
        out_shape=(
            jax.ShapeDtypeStruct((slots, tokens.shape[1]), jnp.bfloat16),
            jax.ShapeDtypeStruct((slots, tokens.shape[0]), jnp.float32),
        ),
        in_specs=[pl.BlockSpec(memory_space=pltpu.SMEM), hbm, hbm, hbm, hbm],
        out_specs=(vmem, vmem),
        scratch_shapes=[
            pltpu.VMEM(ids.shape, ids.dtype),
            pltpu.VMEM(gate_vals.shape, gate_vals.dtype),
            pltpu.VMEM(tokens.shape, tokens.dtype),
            pltpu.VMEM(gain.shape, gain.dtype),
            pltpu.SemaphoreType.DMA((TOKEN_CHUNKS + 3,)),
        ],
        compiler_params=pltpu.CompilerParams(vmem_limit_bytes=VMEM_LIMIT),
        name="pick_rows",
    )(live_counts, *(in_hbm(array) for array in (ids, gate_vals, tokens, gain)))


def expert_rows(rows, gate_ref, up_ref, down_ref):
    dims = (((1,), (1,)), ((), ()))
    gate_act = lax.dot_general(rows, gate_ref[...], dims, preferred_element_type=jnp.float32)
    up_act = lax.dot_general(rows, up_ref[...], dims, preferred_element_type=jnp.float32)
    hidden = (jax.nn.silu(gate_act) * up_act).astype(jnp.bfloat16)
    partial_out = jnp.dot(hidden, down_ref[...], preferred_element_type=jnp.float32)
    return partial_out.astype(jnp.bfloat16)


def expert_blocks(ins, weights, outs):
    together = max(1, 128 // ins[0].shape[0])
    for first in range(0, len(ins), together):
        some = ins[first : first + together]
        partial_out = expert_rows(jnp.concatenate([ref[...] for ref in some], axis=0), *weights)
        at = 0
        for ref in outs[first : first + together]:
            ref[...] = partial_out[at : at + ref.shape[0]]
            at += ref.shape[0]


def expert_cost(blocks, weights):
    size = sum(weight.size for weight in weights)
    rows = sum(block.shape[0] for block in blocks)
    return pl.CostEstimate(flops=2 * rows * size, bytes_accessed=2 * size, transcendentals=0)


def chunk_copies(source, target, chunks, sems):
    rows = source.shape[0] // chunks
    for i in range(chunks):
        at = pl.ds(i * rows, rows)
        yield pltpu.make_async_copy(source.at[at], target.at[at], sems.at[i])


def first_kernel(*refs):
    *refs, sems = refs
    count = (len(refs) - 6) // 2
    ins, sources = refs[:count], refs[count : count + 3]
    outs, weights = refs[count + 3 : 2 * count + 3], refs[2 * count + 3 :]
    copies = [
        copy
        for i, pair in enumerate(zip(sources, weights))
        for copy in chunk_copies(*pair, WEIGHT_CHUNKS, sems.at[i])
    ]
    for copy in copies:
        copy.start()
    for copy in copies:
        copy.wait()
    expert_blocks(ins, weights, outs)


def first_slice(blocks, weights):
    vmem = pl.BlockSpec(memory_space=pltpu.VMEM)
    hbm = pl.BlockSpec(memory_space=pltpu.HBM)
    count = len(blocks)
    outs = pl.pallas_call(
        first_kernel,
        out_shape=[jax.ShapeDtypeStruct(array.shape, array.dtype) for array in (*blocks, *weights)],
        in_specs=[vmem] * count + [hbm] * 3,
        out_specs=[vmem] * (count + 3),
        scratch_shapes=[pltpu.SemaphoreType.DMA((3, WEIGHT_CHUNKS))],
        compiler_params=pltpu.CompilerParams(vmem_limit_bytes=VMEM_LIMIT),
        cost_estimate=expert_cost(blocks, weights),
        name="first_slice",
    )(*blocks, *(in_hbm(weight) for weight in weights))
    return outs[:count], outs[count:]


def last_kernel(*refs):
    count = (len(refs) - 3) // 2
    expert_blocks(refs[:count], refs[count : count + 3], refs[count + 3 :])


def last_slice(blocks, weights):
    vmem = pl.BlockSpec(memory_space=pltpu.VMEM)
    count = len(blocks)
    return pl.pallas_call(
        last_kernel,
        out_shape=[jax.ShapeDtypeStruct(block.shape, jnp.bfloat16) for block in blocks],
        in_specs=[vmem] * (count + 3),
        out_specs=[vmem] * count,
        compiler_params=pltpu.CompilerParams(vmem_limit_bytes=VMEM_LIMIT),
        cost_estimate=expert_cost(blocks, weights),
        name="last_slice",
    )(*blocks, *weights)


def add_level(kept, came):
    return (kept.astype(jnp.float32) + came.astype(jnp.float32)).astype(jnp.bfloat16)


def add_levels(parts):
    while len(parts) > 1:
        parts = [add_level(*pair) for pair in zip(parts[::2], parts[1::2])]
    return parts[0]


def combine_kernel(table_ref, *refs):
    *parts, out_hbm, out_ref, sems = refs
    table = table_ref[...]
    pieces = []
    for _ in range(3):
        pieces.append(table.astype(jnp.bfloat16))
        table = table - pieces[-1].astype(jnp.float32)
    pieces = jnp.concatenate(pieces, axis=0)
    features = out_ref.shape[1]
    width = features // 4
    copies = []
    for i in range(4):
        columns = pl.ds(i * width, width)
        summed = add_levels([part[:, columns] for part in parts])
        out_ref[:, columns] = lax.dot_general(
            pieces,
            jnp.concatenate([summed] * 3, axis=0),
            (((0,), (0,)), ((), ())),
            preferred_element_type=jnp.float32,
        ).astype(jnp.bfloat16)
        copies.append(
            pltpu.make_async_copy(out_ref.at[:, columns], out_hbm.at[:, columns], sems.at[i])
        )
        copies[-1].start()
    for copy in copies:
        copy.wait()


def combine(table, parts):
    vmem = pl.BlockSpec(memory_space=pltpu.VMEM)
    shape = (table.shape[1], parts[0].shape[1])
    return pl.pallas_call(
        combine_kernel,
        out_shape=jax.ShapeDtypeStruct(shape, jnp.bfloat16),
        in_specs=[vmem] * (1 + len(parts)),
        out_specs=pl.BlockSpec(memory_space=pltpu.HBM),
        scratch_shapes=[pltpu.VMEM(shape, jnp.bfloat16), pltpu.SemaphoreType.DMA((4,))],
        compiler_params=pltpu.CompilerParams(vmem_limit_bytes=VMEM_LIMIT),
        name="combine",
    )(table, *parts)


def across_groups(flight, blocks):
    if flight == 1:
        return blocks
    groups = [[g * SLICES + m for g in range(flight)] for m in range(SLICES)]
    return lax.all_to_all(
        blocks, "ep", split_axis=0, concat_axis=0, axis_index_groups=groups, tiled=True
    )


def swap(devices, distance, block):
    return lax.ppermute(block, "ep", [(i, i ^ distance) for i in range(devices)])


def on_device(tokens, norm_gain, expert_ids, gate_vals, live_counts, w_gate, w_up, w_down):
    features = tokens.shape[1]
    devices = lax.axis_size("ep")
    flight = devices // SLICES
    slots = flight * CAP
    rows, table = pick_rows(
        slots, live_counts, expert_ids.T, gate_vals.T, tokens, norm_gain.reshape(1, features)
    )
    own = across_groups(flight, rows)
    near, far, farther = (swap(devices, j, own) for j in (2, 4, 6))
    inner, outer = jnp.concatenate([own, near]), jnp.concatenate([far, farther])
    inner_y, outer_y = swap(devices, 1, inner), swap(devices, 1, outer)
    weights = (w_gate.T, w_up.T, w_down)
    (inner, outer, inner_y), weights = first_slice((inner, outer, inner_y), weights)
    (outer_y,) = last_slice((outer_y,), weights)
    inner, outer = (
        (add_level(kept[:slots], came[:slots]), add_level(kept[slots:], came[slots:]))
        for kept, came in ((inner, swap(devices, 1, inner_y)), (outer, swap(devices, 1, outer_y)))
    )
    parts = [inner[0], swap(devices, 2, inner[1]), swap(devices, 4, outer[0]), swap(devices, 6, outer[1])]
    if flight > 1:
        parts = [across_groups(flight, add_levels(parts))]
    return combine(table, parts)


def solution(mesh):
    return jax.shard_map(
        on_device,
        mesh=mesh,
        in_specs=(
            P(("sp", "ep"), None),
            P(),
            P(("sp", "ep"), None),
            P(("sp", "ep"), None),
            P(("sp", "ep")),
            P(None, "ep"),
            P(None, "ep"),
            P("ep", None),
        ),
        out_specs=P(("sp", "ep"), None),
        check_vma=False,
    )
```

```python
import functools

import jax
import jax.numpy as jnp
from jax import lax
from jax.experimental import pallas as pl
from jax.experimental.pallas import tpu as pltpu
from jax.sharding import PartitionSpec as P

SLICES = 8
CAP = 16
VMEM_LIMIT = 40 * 1024 * 1024
WEIGHT_CHUNKS = 4
TOKEN_CHUNKS = 4


def in_hbm(array):
    return pltpu.with_memory_space_constraint(array, pltpu.HBM)


def pick_kernel(
    live_ref, ids_hbm, gate_hbm, tokens_hbm, gain_hbm, rows_ref, table_ref, ids_ref, gate_ref, tokens_ref, gain_ref, sems
):
    ids_copy, gate_copy, gain_copy = (
        pltpu.make_async_copy(source, target, sems.at[TOKEN_CHUNKS + i])
        for i, (source, target) in enumerate(
            ((ids_hbm, ids_ref), (gate_hbm, gate_ref), (gain_hbm, gain_ref))
        )
    )
    token_copies = list(chunk_copies(tokens_hbm, tokens_ref, TOKEN_CHUNKS, sems))
    for copy in (ids_copy, *token_copies, gain_copy, gate_copy):
        copy.start()
    slots, tok_rows = table_ref.shape
    slot = lax.broadcasted_iota(jnp.int32, (slots, tok_rows), 0)
    token = lax.broadcasted_iota(jnp.int32, (slots, tok_rows), 1)
    expert, place = slot // CAP, slot % CAP
    live = token < live_ref[0]
    before = lax.broadcasted_iota(jnp.int32, (tok_rows, tok_rows), 0)
    after = lax.broadcasted_iota(jnp.int32, (tok_rows, tok_rows), 1)
    earlier = jnp.where(before < after, 1.0, 0.0).astype(jnp.bfloat16)
    ids_copy.wait()
    hits = [(ids_ref[k : k + 1, :] == expert) & live for k in range(ids_ref.shape[0])]
    chosen = jnp.where(functools.reduce(jnp.logical_or, hits), 1.0, 0.0)
    rank = jnp.dot(chosen.astype(jnp.bfloat16), earlier, preferred_element_type=jnp.float32)
    pick = jnp.where((chosen > 0.0) & (rank.astype(jnp.int32) == place), 1.0, 0.0)
    for copy in token_copies:
        copy.wait()
    values = jnp.dot(pick.astype(jnp.bfloat16), tokens_ref[...], preferred_element_type=jnp.float32)
    mean_sq = jnp.mean(values * values, axis=-1, keepdims=True)
    gain_copy.wait()
    rows_ref[...] = (values * lax.rsqrt(mean_sq + 1e-06) * gain_ref[...]).astype(jnp.bfloat16)
    gate_copy.wait()
    weight = jnp.zeros((slots, tok_rows), jnp.float32)
    for k, hit in enumerate(hits):
        weight = jnp.where(hit, gate_ref[k : k + 1, :], weight)
    table_ref[...] = pick * weight


def pick_rows(slots, live_counts, ids, gate_vals, tokens, gain):
    vmem = pl.BlockSpec(memory_space=pltpu.VMEM)
    hbm = pl.BlockSpec(memory_space=pltpu.HBM)
    return pl.pallas_call(
        pick_kernel,
        out_shape=(
            jax.ShapeDtypeStruct((slots, tokens.shape[1]), jnp.bfloat16),
            jax.ShapeDtypeStruct((slots, tokens.shape[0]), jnp.float32),
        ),
        in_specs=[pl.BlockSpec(memory_space=pltpu.SMEM), hbm, hbm, hbm, hbm],
        out_specs=(vmem, vmem),
        scratch_shapes=[
            pltpu.VMEM(ids.shape, ids.dtype),
            pltpu.VMEM(gate_vals.shape, gate_vals.dtype),
            pltpu.VMEM(tokens.shape, tokens.dtype),
            pltpu.VMEM(gain.shape, gain.dtype),
            pltpu.SemaphoreType.DMA((TOKEN_CHUNKS + 3,)),
        ],
        compiler_params=pltpu.CompilerParams(vmem_limit_bytes=VMEM_LIMIT),
        name="pick_rows",
    )(live_counts, *(in_hbm(array) for array in (ids, gate_vals, tokens, gain)))


def expert_rows(rows, gate_ref, up_ref, down_ref):
    dims = (((1,), (1,)), ((), ()))
    gate_act = lax.dot_general(rows, gate_ref[...], dims, preferred_element_type=jnp.float32)
    up_act = lax.dot_general(rows, up_ref[...], dims, preferred_element_type=jnp.float32)
    hidden = (jax.nn.silu(gate_act) * up_act).astype(jnp.bfloat16)
    partial_out = jnp.dot(hidden, down_ref[...], preferred_element_type=jnp.float32)
    return partial_out.astype(jnp.bfloat16)


def expert_blocks(ins, weights, outs):
    together = max(1, 128 // ins[0].shape[0])
    for first in range(0, len(ins), together):
        some = ins[first : first + together]
        partial_out = expert_rows(jnp.concatenate([ref[...] for ref in some], axis=0), *weights)
        at = 0
        for ref in outs[first : first + together]:
            ref[...] = partial_out[at : at + ref.shape[0]]
            at += ref.shape[0]


def expert_cost(blocks, weights):
    size = sum(weight.size for weight in weights)
    rows = sum(block.shape[0] for block in blocks)
    return pl.CostEstimate(flops=2 * rows * size, bytes_accessed=2 * size, transcendentals=0)


def chunk_copies(source, target, chunks, sems):
    rows = source.shape[0] // chunks
    for i in range(chunks):
        at = pl.ds(i * rows, rows)
        yield pltpu.make_async_copy(source.at[at], target.at[at], sems.at[i])


def stage_kernel(rows_ref, *refs):
    *refs, sems = refs
    sources, out_ref, weights = refs[:3], refs[3], refs[4:]
    copies = [
        copy
        for i, pair in enumerate(zip(sources, weights))
        for copy in chunk_copies(*pair, WEIGHT_CHUNKS, sems.at[i])
    ]
    for copy in copies:
        copy.start()
    out_ref[...] = rows_ref[...]
    for copy in copies:
        copy.wait()


def stage_weights(rows, weights):
    vmem = pl.BlockSpec(memory_space=pltpu.VMEM)
    hbm = pl.BlockSpec(memory_space=pltpu.HBM)
    rows, *weights = pl.pallas_call(
        stage_kernel,
        out_shape=[jax.ShapeDtypeStruct(array.shape, array.dtype) for array in (rows, *weights)],
        in_specs=[vmem] + [hbm] * 3,
        out_specs=[vmem] * 4,
        scratch_shapes=[pltpu.SemaphoreType.DMA((3, WEIGHT_CHUNKS))],
        compiler_params=pltpu.CompilerParams(vmem_limit_bytes=VMEM_LIMIT),
        cost_estimate=expert_cost([rows], weights),
        name="stage_weights",
    )(rows, *(in_hbm(weight) for weight in weights))
    return rows, weights


def slice_kernel(*refs):
    count = (len(refs) - 3) // 2
    expert_blocks(refs[:count], refs[count : count + 3], refs[count + 3 :])


def expert_slice(blocks, weights):
    vmem = pl.BlockSpec(memory_space=pltpu.VMEM)
    count = len(blocks)
    return pl.pallas_call(
        slice_kernel,
        out_shape=[jax.ShapeDtypeStruct(block.shape, jnp.bfloat16) for block in blocks],
        in_specs=[vmem] * (count + 3),
        out_specs=[vmem] * count,
        compiler_params=pltpu.CompilerParams(vmem_limit_bytes=VMEM_LIMIT),
        cost_estimate=expert_cost(blocks, weights),
        name="expert_slice",
    )(*blocks, *weights)


def add_level(kept, came):
    return (kept.astype(jnp.float32) + came.astype(jnp.float32)).astype(jnp.bfloat16)


def combine_kernel(table_ref, *refs):
    *parts, out_hbm, out_ref, sems = refs
    table = table_ref[...]
    pieces = []
    for _ in range(3):
        pieces.append(table.astype(jnp.bfloat16))
        table = table - pieces[-1].astype(jnp.float32)
    pieces = jnp.concatenate(pieces, axis=0)
    features = out_ref.shape[1]
    width = features // 4
    copies = []
    for i in range(4):
        columns = pl.ds(i * width, width)
        summed = functools.reduce(add_level, [part[:, columns] for part in parts])
        out_ref[:, columns] = lax.dot_general(
            pieces,
            jnp.concatenate([summed] * 3, axis=0),
            (((0,), (0,)), ((), ())),
            preferred_element_type=jnp.float32,
        ).astype(jnp.bfloat16)
        copies.append(
            pltpu.make_async_copy(out_ref.at[:, columns], out_hbm.at[:, columns], sems.at[i])
        )
        copies[-1].start()
    for copy in copies:
        copy.wait()


def combine(table, parts):
    vmem = pl.BlockSpec(memory_space=pltpu.VMEM)
    shape = (table.shape[1], parts[0].shape[1])
    return pl.pallas_call(
        combine_kernel,
        out_shape=jax.ShapeDtypeStruct(shape, jnp.bfloat16),
        in_specs=[vmem] * (1 + len(parts)),
        out_specs=pl.BlockSpec(memory_space=pltpu.HBM),
        scratch_shapes=[pltpu.VMEM(shape, jnp.bfloat16), pltpu.SemaphoreType.DMA((4,))],
        compiler_params=pltpu.CompilerParams(vmem_limit_bytes=VMEM_LIMIT),
        name="combine",
    )(table, *parts)


def across_groups(flight, blocks):
    if flight == 1:
        return blocks
    groups = [[g * SLICES + m for g in range(flight)] for m in range(SLICES)]
    return lax.all_to_all(
        blocks, "ep", split_axis=0, concat_axis=0, axis_index_groups=groups, tiled=True
    )


def swap(devices, distance, block):
    return lax.ppermute(block, "ep", [(i, i ^ distance) for i in range(devices)])


def on_device(tokens, norm_gain, expert_ids, gate_vals, live_counts, w_gate, w_up, w_down):
    features = tokens.shape[1]
    devices = lax.axis_size("ep")
    flight = devices // SLICES
    slots = flight * CAP
    rows, table = pick_rows(
        slots, live_counts, expert_ids.T, gate_vals.T, tokens, norm_gain.reshape(1, features)
    )
    own = across_groups(flight, rows)
    far = swap(devices, 4, own)
    own, weights = stage_weights(own, (w_gate.T, w_up.T, w_down))
    near = swap(devices, 2, own)
    farther = swap(devices, 2, far)
    inner, outer = jnp.concatenate([own, near]), jnp.concatenate([far, farther])
    inner_y, outer_y = swap(devices, 1, inner), swap(devices, 1, outer)
    inner, outer, inner_y = expert_slice((inner, outer, inner_y), weights)
    (outer_y,) = expert_slice((outer_y,), weights)
    inner_y, outer_y = swap(devices, 1, inner_y), swap(devices, 1, outer_y)
    own, near = (add_level(inner[at], inner_y[at]) for at in (slice(slots), slice(slots, None)))
    far, farther = (add_level(outer[at], outer_y[at]) for at in (slice(slots), slice(slots, None)))
    near = swap(devices, 2, near)
    far = swap(devices, 4, add_level(far, swap(devices, 2, farther)))
    parts = [own, near, far]
    if flight > 1:
        parts = [across_groups(flight, functools.reduce(add_level, parts))]
    return combine(table, parts)


def solution(mesh):
    return jax.shard_map(
        on_device,
        mesh=mesh,
        in_specs=(
            P(("sp", "ep"), None),
            P(),
            P(("sp", "ep"), None),
            P(("sp", "ep"), None),
            P(("sp", "ep")),
            P(None, "ep"),
            P(None, "ep"),
            P("ep", None),
        ),
        out_specs=P(("sp", "ep"), None),
        check_vma=False,
    )
```

```python
import functools

import jax
import jax.numpy as jnp
from jax import lax
from jax.experimental import pallas as pl
from jax.experimental.pallas import tpu as pltpu
from jax.sharding import PartitionSpec as P

SLICES = 8
CAP = 16
VMEM_LIMIT = 40 * 1024 * 1024
WEIGHT_CHUNKS = 4
TOKEN_CHUNKS = 4


def in_hbm(array):
    return pltpu.with_memory_space_constraint(array, pltpu.HBM)


def pick_kernel(
    live_ref, ids_hbm, gate_hbm, tokens_hbm, gain_hbm, rows_ref, table_ref, ids_ref, gate_ref, tokens_ref, gain_ref, sems
):
    ids_copy, gate_copy, gain_copy = (
        pltpu.make_async_copy(source, target, sems.at[TOKEN_CHUNKS + i])
        for i, (source, target) in enumerate(
            ((ids_hbm, ids_ref), (gate_hbm, gate_ref), (gain_hbm, gain_ref))
        )
    )
    token_copies = list(chunk_copies(tokens_hbm, tokens_ref, TOKEN_CHUNKS, sems))
    for copy in (ids_copy, *token_copies, gain_copy, gate_copy):
        copy.start()
    slots, tok_rows = table_ref.shape
    slot = lax.broadcasted_iota(jnp.int32, (slots, tok_rows), 0)
    token = lax.broadcasted_iota(jnp.int32, (slots, tok_rows), 1)
    expert, place = slot // CAP, slot % CAP
    live = token < live_ref[0]
    before = lax.broadcasted_iota(jnp.int32, (tok_rows, tok_rows), 0)
    after = lax.broadcasted_iota(jnp.int32, (tok_rows, tok_rows), 1)
    earlier = jnp.where(before < after, 1.0, 0.0).astype(jnp.bfloat16)
    ids_copy.wait()
    hits = [(ids_ref[k : k + 1, :] == expert) & live for k in range(ids_ref.shape[0])]
    chosen = jnp.where(functools.reduce(jnp.logical_or, hits), 1.0, 0.0)
    rank = jnp.dot(chosen.astype(jnp.bfloat16), earlier, preferred_element_type=jnp.float32)
    pick = jnp.where((chosen > 0.0) & (rank.astype(jnp.int32) == place), 1.0, 0.0)
    for copy in token_copies:
        copy.wait()
    values = jnp.dot(pick.astype(jnp.bfloat16), tokens_ref[...], preferred_element_type=jnp.float32)
    mean_sq = jnp.mean(values * values, axis=-1, keepdims=True)
    gain_copy.wait()
    rows_ref[...] = (values * lax.rsqrt(mean_sq + 1e-06) * gain_ref[...]).astype(jnp.bfloat16)
    gate_copy.wait()
    weight = jnp.zeros((slots, tok_rows), jnp.float32)
    for k, hit in enumerate(hits):
        weight = jnp.where(hit, gate_ref[k : k + 1, :], weight)
    table_ref[...] = pick * weight


def pick_rows(slots, live_counts, ids, gate_vals, tokens, gain):
    vmem = pl.BlockSpec(memory_space=pltpu.VMEM)
    hbm = pl.BlockSpec(memory_space=pltpu.HBM)
    return pl.pallas_call(
        pick_kernel,
        out_shape=(
            jax.ShapeDtypeStruct((slots, tokens.shape[1]), jnp.bfloat16),
            jax.ShapeDtypeStruct((slots, tokens.shape[0]), jnp.float32),
        ),
        in_specs=[pl.BlockSpec(memory_space=pltpu.SMEM), hbm, hbm, hbm, hbm],
        out_specs=(vmem, vmem),
        scratch_shapes=[
            pltpu.VMEM(ids.shape, ids.dtype),
            pltpu.VMEM(gate_vals.shape, gate_vals.dtype),
            pltpu.VMEM(tokens.shape, tokens.dtype),
            pltpu.VMEM(gain.shape, gain.dtype),
            pltpu.SemaphoreType.DMA((TOKEN_CHUNKS + 3,)),
        ],
        compiler_params=pltpu.CompilerParams(vmem_limit_bytes=VMEM_LIMIT),
        name="pick_rows",
    )(live_counts, *(in_hbm(array) for array in (ids, gate_vals, tokens, gain)))


def expert_rows(rows, gate_ref, up_ref, down_ref):
    dims = (((1,), (1,)), ((), ()))
    gate_act = lax.dot_general(rows, gate_ref[...], dims, preferred_element_type=jnp.float32)
    up_act = lax.dot_general(rows, up_ref[...], dims, preferred_element_type=jnp.float32)
    hidden = (jax.nn.silu(gate_act) * up_act).astype(jnp.bfloat16)
    partial_out = jnp.dot(hidden, down_ref[...], preferred_element_type=jnp.float32)
    return partial_out.astype(jnp.bfloat16)


def expert_blocks(ins, weights, outs):
    together = max(1, 128 // ins[0].shape[0])
    for first in range(0, len(ins), together):
        some = ins[first : first + together]
        partial_out = expert_rows(jnp.concatenate([ref[...] for ref in some], axis=0), *weights)
        at = 0
        for ref in outs[first : first + together]:
            ref[...] = partial_out[at : at + ref.shape[0]]
            at += ref.shape[0]


def expert_cost(blocks, weights):
    size = sum(weight.size for weight in weights)
    rows = sum(block.shape[0] for block in blocks)
    return pl.CostEstimate(flops=2 * rows * size, bytes_accessed=2 * size, transcendentals=0)


def chunk_copies(source, target, chunks, sems):
    rows = source.shape[0] // chunks
    for i in range(chunks):
        at = pl.ds(i * rows, rows)
        yield pltpu.make_async_copy(source.at[at], target.at[at], sems.at[i])


def stage_kernel(rows_ref, *refs):
    *refs, sems = refs
    sources, out_ref, weights = refs[:3], refs[3], refs[4:]
    copies = [
        copy
        for i, pair in enumerate(zip(sources, weights))
        for copy in chunk_copies(*pair, WEIGHT_CHUNKS, sems.at[i])
    ]
    for copy in copies:
        copy.start()
    out_ref[...] = rows_ref[...]
    for copy in copies:
        copy.wait()


def stage_weights(rows, weights):
    vmem = pl.BlockSpec(memory_space=pltpu.VMEM)
    hbm = pl.BlockSpec(memory_space=pltpu.HBM)
    rows, *weights = pl.pallas_call(
        stage_kernel,
        out_shape=[jax.ShapeDtypeStruct(array.shape, array.dtype) for array in (rows, *weights)],
        in_specs=[vmem] + [hbm] * 3,
        out_specs=[vmem] * 4,
        scratch_shapes=[pltpu.SemaphoreType.DMA((3, WEIGHT_CHUNKS))],
        compiler_params=pltpu.CompilerParams(vmem_limit_bytes=VMEM_LIMIT),
        cost_estimate=expert_cost([rows], weights),
        name="stage_weights",
    )(rows, *(in_hbm(weight) for weight in weights))
    return rows, weights


def slice_kernel(count, *refs):
    outs = refs[len(refs) - count :]
    expert_blocks(refs[:count], refs[count : count + 3], outs)


def expert_slice(blocks, weights, after=()):
    vmem = pl.BlockSpec(memory_space=pltpu.VMEM)
    count = len(blocks)
    return pl.pallas_call(
        functools.partial(slice_kernel, count),
        out_shape=[jax.ShapeDtypeStruct(block.shape, jnp.bfloat16) for block in blocks],
        in_specs=[vmem] * (count + 3) + [pl.BlockSpec(memory_space=pl.ANY)] * len(after),
        out_specs=[vmem] * count,
        compiler_params=pltpu.CompilerParams(vmem_limit_bytes=VMEM_LIMIT),
        cost_estimate=expert_cost(blocks, weights),
        name="expert_slice",
    )(*blocks, *weights, *after)


def add_level(kept, came):
    return (kept.astype(jnp.float32) + came.astype(jnp.float32)).astype(jnp.bfloat16)


def combine_kernel(table_ref, *refs):
    *parts, out_hbm, out_ref, sems = refs
    table = table_ref[...]
    pieces = []
    for _ in range(3):
        pieces.append(table.astype(jnp.bfloat16))
        table = table - pieces[-1].astype(jnp.float32)
    pieces = jnp.concatenate(pieces, axis=0)
    features = out_ref.shape[1]
    width = features // 4
    copies = []
    for i in range(4):
        columns = pl.ds(i * width, width)
        summed = functools.reduce(add_level, [part[:, columns] for part in parts])
        out_ref[:, columns] = lax.dot_general(
            pieces,
            jnp.concatenate([summed] * 3, axis=0),
            (((0,), (0,)), ((), ())),
            preferred_element_type=jnp.float32,
        ).astype(jnp.bfloat16)
        copies.append(
            pltpu.make_async_copy(out_ref.at[:, columns], out_hbm.at[:, columns], sems.at[i])
        )
        copies[-1].start()
    for copy in copies:
        copy.wait()


def combine(table, parts):
    vmem = pl.BlockSpec(memory_space=pltpu.VMEM)
    shape = (table.shape[1], parts[0].shape[1])
    return pl.pallas_call(
        combine_kernel,
        out_shape=jax.ShapeDtypeStruct(shape, jnp.bfloat16),
        in_specs=[vmem] * (1 + len(parts)),
        out_specs=pl.BlockSpec(memory_space=pltpu.HBM),
        scratch_shapes=[pltpu.VMEM(shape, jnp.bfloat16), pltpu.SemaphoreType.DMA((4,))],
        compiler_params=pltpu.CompilerParams(vmem_limit_bytes=VMEM_LIMIT),
        name="combine",
    )(table, *parts)


def across_groups(flight, blocks):
    if flight == 1:
        return blocks
    groups = [[g * SLICES + m for g in range(flight)] for m in range(SLICES)]
    return lax.all_to_all(
        blocks, "ep", split_axis=0, concat_axis=0, axis_index_groups=groups, tiled=True
    )


def swap(devices, distance, block):
    return lax.ppermute(block, "ep", [(i, i ^ distance) for i in range(devices)])


def on_device(tokens, norm_gain, expert_ids, gate_vals, live_counts, w_gate, w_up, w_down):
    features = tokens.shape[1]
    devices = lax.axis_size("ep")
    flight = devices // SLICES
    slots = flight * CAP
    rows, table = pick_rows(
        slots, live_counts, expert_ids.T, gate_vals.T, tokens, norm_gain.reshape(1, features)
    )
    own = across_groups(flight, rows)
    farther, far = swap(devices, 6, own), swap(devices, 4, own)
    own, weights = stage_weights(own, (w_gate.T, w_up.T, w_down))
    near = swap(devices, 2, own)
    outer, inner = jnp.concatenate([far, farther]), jnp.concatenate([own, near])
    outer_y, inner_y = swap(devices, 1, outer), swap(devices, 1, inner)
    (outer_y,) = expert_slice((outer_y,), weights)
    outer, inner, inner_y = expert_slice((outer, inner, inner_y), weights, (outer_y,))
    outer_y, inner_y = swap(devices, 1, outer_y), swap(devices, 1, inner_y)
    far, farther = (add_level(outer[at], outer_y[at]) for at in (slice(slots), slice(slots, None)))
    own, near = (add_level(inner[at], inner_y[at]) for at in (slice(slots), slice(slots, None)))
    farther, far = swap(devices, 6, farther), swap(devices, 4, far)
    parts = [own, swap(devices, 2, near), add_level(far, farther)]
    if flight > 1:
        parts = [across_groups(flight, functools.reduce(add_level, parts))]
    return combine(table, parts)


def solution(mesh):
    return jax.shard_map(
        on_device,
        mesh=mesh,
        in_specs=(
            P(("sp", "ep"), None),
            P(),
            P(("sp", "ep"), None),
            P(("sp", "ep"), None),
            P(("sp", "ep")),
            P(None, "ep"),
            P(None, "ep"),
            P("ep", None),
        ),
        out_specs=P(("sp", "ep"), None),
        check_vma=False,
    )
```

```python
import functools

import jax
import jax.numpy as jnp
from jax import lax
from jax.experimental import pallas as pl
from jax.experimental.pallas import tpu as pltpu
from jax.sharding import PartitionSpec as P

SLICES = 8
CAP = 16
VMEM_LIMIT = 40 * 1024 * 1024
WEIGHT_CHUNKS = 4
TOKEN_CHUNKS = 4


def in_hbm(array):
    return pltpu.with_memory_space_constraint(array, pltpu.HBM)


def pick_kernel(
    live_ref, ids_hbm, gate_hbm, tokens_hbm, gain_hbm, rows_ref, table_ref, ids_ref, gate_ref, tokens_ref, gain_ref, sems
):
    ids_copy, gate_copy, gain_copy = (
        pltpu.make_async_copy(source, target, sems.at[TOKEN_CHUNKS + i])
        for i, (source, target) in enumerate(
            ((ids_hbm, ids_ref), (gate_hbm, gate_ref), (gain_hbm, gain_ref))
        )
    )
    token_copies = list(chunk_copies(tokens_hbm, tokens_ref, TOKEN_CHUNKS, sems))
    for copy in (ids_copy, *token_copies, gain_copy, gate_copy):
        copy.start()
    slots, tok_rows = table_ref.shape
    slot = lax.broadcasted_iota(jnp.int32, (slots, tok_rows), 0)
    token = lax.broadcasted_iota(jnp.int32, (slots, tok_rows), 1)
    expert, place = slot // CAP, slot % CAP
    live = token < live_ref[0]
    before = lax.broadcasted_iota(jnp.int32, (tok_rows, tok_rows), 0)
    after = lax.broadcasted_iota(jnp.int32, (tok_rows, tok_rows), 1)
    earlier = jnp.where(before < after, 1.0, 0.0).astype(jnp.bfloat16)
    ids_copy.wait()
    hits = [(ids_ref[k : k + 1, :] == expert) & live for k in range(ids_ref.shape[0])]
    chosen = jnp.where(functools.reduce(jnp.logical_or, hits), 1.0, 0.0)
    rank = jnp.dot(chosen.astype(jnp.bfloat16), earlier, preferred_element_type=jnp.float32)
    pick = jnp.where((chosen > 0.0) & (rank.astype(jnp.int32) == place), 1.0, 0.0)
    for copy in token_copies:
        copy.wait()
    values = jnp.dot(pick.astype(jnp.bfloat16), tokens_ref[...], preferred_element_type=jnp.float32)
    mean_sq = jnp.mean(values * values, axis=-1, keepdims=True)
    gain_copy.wait()
    rows_ref[...] = (values * lax.rsqrt(mean_sq + 1e-06) * gain_ref[...]).astype(jnp.bfloat16)
    gate_copy.wait()
    weight = jnp.zeros((slots, tok_rows), jnp.float32)
    for k, hit in enumerate(hits):
        weight = jnp.where(hit, gate_ref[k : k + 1, :], weight)
    table_ref[...] = pick * weight


def pick_rows(slots, live_counts, ids, gate_vals, tokens, gain):
    vmem = pl.BlockSpec(memory_space=pltpu.VMEM)
    hbm = pl.BlockSpec(memory_space=pltpu.HBM)
    return pl.pallas_call(
        pick_kernel,
        out_shape=(
            jax.ShapeDtypeStruct((slots, tokens.shape[1]), jnp.bfloat16),
            jax.ShapeDtypeStruct((slots, tokens.shape[0]), jnp.float32),
        ),
        in_specs=[pl.BlockSpec(memory_space=pltpu.SMEM), hbm, hbm, hbm, hbm],
        out_specs=(vmem, vmem),
        scratch_shapes=[
            pltpu.VMEM(ids.shape, ids.dtype),
            pltpu.VMEM(gate_vals.shape, gate_vals.dtype),
            pltpu.VMEM(tokens.shape, tokens.dtype),
            pltpu.VMEM(gain.shape, gain.dtype),
            pltpu.SemaphoreType.DMA((TOKEN_CHUNKS + 3,)),
        ],
        compiler_params=pltpu.CompilerParams(vmem_limit_bytes=VMEM_LIMIT),
        name="pick_rows",
    )(live_counts, *(in_hbm(array) for array in (ids, gate_vals, tokens, gain)))


def expert_rows(rows, gate_ref, up_ref, down_ref):
    dims = (((1,), (1,)), ((), ()))
    gate_act = lax.dot_general(rows, gate_ref[...], dims, preferred_element_type=jnp.float32)
    up_act = lax.dot_general(rows, up_ref[...], dims, preferred_element_type=jnp.float32)
    hidden = (jax.nn.silu(gate_act) * up_act).astype(jnp.bfloat16)
    partial_out = jnp.dot(hidden, down_ref[...], preferred_element_type=jnp.float32)
    return partial_out.astype(jnp.bfloat16)


def expert_blocks(ins, weights, outs):
    together = max(1, 128 // ins[0].shape[0])
    for first in range(0, len(ins), together):
        some = ins[first : first + together]
        partial_out = expert_rows(jnp.concatenate([ref[...] for ref in some], axis=0), *weights)
        at = 0
        for ref in outs[first : first + together]:
            ref[...] = partial_out[at : at + ref.shape[0]]
            at += ref.shape[0]


def expert_cost(blocks, weights):
    size = sum(weight.size for weight in weights)
    rows = sum(block.shape[0] for block in blocks)
    return pl.CostEstimate(flops=2 * rows * size, bytes_accessed=2 * size, transcendentals=0)


def chunk_copies(source, target, chunks, sems):
    rows = source.shape[0] // chunks
    for i in range(chunks):
        at = pl.ds(i * rows, rows)
        yield pltpu.make_async_copy(source.at[at], target.at[at], sems.at[i])


def stage_kernel(rows_ref, *refs):
    *refs, sems = refs
    sources, out_ref, weights = refs[:3], refs[3], refs[4:]
    copies = [
        copy
        for i, pair in enumerate(zip(sources, weights))
        for copy in chunk_copies(*pair, WEIGHT_CHUNKS, sems.at[i])
    ]
    for copy in copies:
        copy.start()
    out_ref[...] = rows_ref[...]
    for copy in copies:
        copy.wait()


def stage_weights(rows, weights):
    vmem = pl.BlockSpec(memory_space=pltpu.VMEM)
    hbm = pl.BlockSpec(memory_space=pltpu.HBM)
    rows, *weights = pl.pallas_call(
        stage_kernel,
        out_shape=[jax.ShapeDtypeStruct(array.shape, array.dtype) for array in (rows, *weights)],
        in_specs=[vmem] + [hbm] * 3,
        out_specs=[vmem] * 4,
        scratch_shapes=[pltpu.SemaphoreType.DMA((3, WEIGHT_CHUNKS))],
        compiler_params=pltpu.CompilerParams(vmem_limit_bytes=VMEM_LIMIT),
        cost_estimate=expert_cost([rows], weights),
        name="stage_weights",
    )(rows, *(in_hbm(weight) for weight in weights))
    return rows, weights


def slice_kernel(count, *refs):
    outs = refs[len(refs) - count :]
    expert_blocks(refs[:count], refs[count : count + 3], outs)


def expert_slice(blocks, weights, after=()):
    vmem = pl.BlockSpec(memory_space=pltpu.VMEM)
    count = len(blocks)
    return pl.pallas_call(
        functools.partial(slice_kernel, count),
        out_shape=[jax.ShapeDtypeStruct(block.shape, jnp.bfloat16) for block in blocks],
        in_specs=[vmem] * (count + 3) + [pl.BlockSpec(memory_space=pl.ANY)] * len(after),
        out_specs=[vmem] * count,
        compiler_params=pltpu.CompilerParams(vmem_limit_bytes=VMEM_LIMIT),
        cost_estimate=expert_cost(blocks, weights),
        name="expert_slice",
    )(*blocks, *weights, *after)


def add_level(kept, came):
    return (kept.astype(jnp.float32) + came.astype(jnp.float32)).astype(jnp.bfloat16)


def combine_kernel(table_ref, *refs):
    *parts, out_hbm, out_ref, sems = refs
    table = table_ref[...]
    pieces = []
    for _ in range(3):
        pieces.append(table.astype(jnp.bfloat16))
        table = table - pieces[-1].astype(jnp.float32)
    pieces = jnp.concatenate(pieces, axis=0)
    features = out_ref.shape[1]
    width = features // 4
    copies = []
    for i in range(4):
        columns = pl.ds(i * width, width)
        summed = functools.reduce(add_level, [part[:, columns] for part in parts])
        out_ref[:, columns] = lax.dot_general(
            pieces,
            jnp.concatenate([summed] * 3, axis=0),
            (((0,), (0,)), ((), ())),
            preferred_element_type=jnp.float32,
        ).astype(jnp.bfloat16)
        copies.append(
            pltpu.make_async_copy(out_ref.at[:, columns], out_hbm.at[:, columns], sems.at[i])
        )
        copies[-1].start()
    for copy in copies:
        copy.wait()


def combine(table, parts):
    vmem = pl.BlockSpec(memory_space=pltpu.VMEM)
    shape = (table.shape[1], parts[0].shape[1])
    return pl.pallas_call(
        combine_kernel,
        out_shape=jax.ShapeDtypeStruct(shape, jnp.bfloat16),
        in_specs=[vmem] * (1 + len(parts)),
        out_specs=pl.BlockSpec(memory_space=pltpu.HBM),
        scratch_shapes=[pltpu.VMEM(shape, jnp.bfloat16), pltpu.SemaphoreType.DMA((4,))],
        compiler_params=pltpu.CompilerParams(vmem_limit_bytes=VMEM_LIMIT),
        name="combine",
    )(table, *parts)


def across_groups(flight, blocks):
    if flight == 1:
        return blocks
    groups = [[g * SLICES + m for g in range(flight)] for m in range(SLICES)]
    return lax.all_to_all(
        blocks, "ep", split_axis=0, concat_axis=0, axis_index_groups=groups, tiled=True
    )


def swap(devices, distance, block):
    return lax.ppermute(block, "ep", [(i, i ^ distance) for i in range(devices)])


def on_device(tokens, norm_gain, expert_ids, gate_vals, live_counts, w_gate, w_up, w_down):
    features = tokens.shape[1]
    devices = lax.axis_size("ep")
    flight = devices // SLICES
    slots = flight * CAP
    rows, table = pick_rows(
        slots, live_counts, expert_ids.T, gate_vals.T, tokens, norm_gain.reshape(1, features)
    )
    own = across_groups(flight, rows)
    weights = (w_gate.T, w_up.T, w_down)
    own, weights = stage_weights(own, weights)
    groups = [[g * SLICES + m for m in range(SLICES)] for g in range(flight)]
    groups = None if flight == 1 else groups
    arrived = lax.all_gather(own, "ep", axis_index_groups=groups, tiled=True)
    (partial_out,) = expert_slice((arrived,), weights)
    summed = lax.psum_scatter(
        partial_out, "ep", scatter_dimension=0, axis_index_groups=groups, tiled=True
    )
    parts = [across_groups(flight, summed)]
    return combine(table, parts)


def solution(mesh):
    return jax.shard_map(
        on_device,
        mesh=mesh,
        in_specs=(
            P(("sp", "ep"), None),
            P(),
            P(("sp", "ep"), None),
            P(("sp", "ep"), None),
            P(("sp", "ep")),
            P(None, "ep"),
            P(None, "ep"),
            P("ep", None),
        ),
        out_specs=P(("sp", "ep"), None),
        check_vma=False,
    )
```

```python
import functools

import jax
import jax.numpy as jnp
from jax import lax
from jax.experimental import pallas as pl
from jax.experimental.pallas import tpu as pltpu
from jax.sharding import PartitionSpec as P

SLICES = 8
CAP = 16
VMEM_LIMIT = 40 * 1024 * 1024
WEIGHT_CHUNKS = 4
TOKEN_CHUNKS = 4


def in_hbm(array):
    return pltpu.with_memory_space_constraint(array, pltpu.HBM)


def pick_kernel(
    live_ref, ids_hbm, gate_hbm, tokens_hbm, gain_hbm, rows_ref, table_ref, ids_ref, gate_ref, tokens_ref, gain_ref, sems
):
    ids_copy, gate_copy, gain_copy = (
        pltpu.make_async_copy(source, target, sems.at[TOKEN_CHUNKS + i])
        for i, (source, target) in enumerate(
            ((ids_hbm, ids_ref), (gate_hbm, gate_ref), (gain_hbm, gain_ref))
        )
    )
    token_copies = list(chunk_copies(tokens_hbm, tokens_ref, TOKEN_CHUNKS, sems))
    for copy in (ids_copy, *token_copies, gain_copy, gate_copy):
        copy.start()
    slots, tok_rows = table_ref.shape
    slot = lax.broadcasted_iota(jnp.int32, (slots, tok_rows), 0)
    token = lax.broadcasted_iota(jnp.int32, (slots, tok_rows), 1)
    expert, place = slot // CAP, slot % CAP
    live = token < live_ref[0]
    before = lax.broadcasted_iota(jnp.int32, (tok_rows, tok_rows), 0)
    after = lax.broadcasted_iota(jnp.int32, (tok_rows, tok_rows), 1)
    earlier = jnp.where(before < after, 1.0, 0.0).astype(jnp.bfloat16)
    ids_copy.wait()
    hits = [(ids_ref[k : k + 1, :] == expert) & live for k in range(ids_ref.shape[0])]
    chosen = jnp.where(functools.reduce(jnp.logical_or, hits), 1.0, 0.0)
    rank = jnp.dot(chosen.astype(jnp.bfloat16), earlier, preferred_element_type=jnp.float32)
    pick = jnp.where((chosen > 0.0) & (rank.astype(jnp.int32) == place), 1.0, 0.0)
    for copy in token_copies:
        copy.wait()
    values = jnp.dot(pick.astype(jnp.bfloat16), tokens_ref[...], preferred_element_type=jnp.float32)
    mean_sq = jnp.mean(values * values, axis=-1, keepdims=True)
    gain_copy.wait()
    rows_ref[...] = (values * lax.rsqrt(mean_sq + 1e-06) * gain_ref[...]).astype(jnp.bfloat16)
    gate_copy.wait()
    weight = jnp.zeros((slots, tok_rows), jnp.float32)
    for k, hit in enumerate(hits):
        weight = jnp.where(hit, gate_ref[k : k + 1, :], weight)
    table_ref[...] = pick * weight


def pick_rows(slots, live_counts, ids, gate_vals, tokens, gain):
    vmem = pl.BlockSpec(memory_space=pltpu.VMEM)
    hbm = pl.BlockSpec(memory_space=pltpu.HBM)
    return pl.pallas_call(
        pick_kernel,
        out_shape=(
            jax.ShapeDtypeStruct((slots, tokens.shape[1]), jnp.bfloat16),
            jax.ShapeDtypeStruct((slots, tokens.shape[0]), jnp.float32),
        ),
        in_specs=[pl.BlockSpec(memory_space=pltpu.SMEM), hbm, hbm, hbm, hbm],
        out_specs=(vmem, vmem),
        scratch_shapes=[
            pltpu.VMEM(ids.shape, ids.dtype),
            pltpu.VMEM(gate_vals.shape, gate_vals.dtype),
            pltpu.VMEM(tokens.shape, tokens.dtype),
            pltpu.VMEM(gain.shape, gain.dtype),
            pltpu.SemaphoreType.DMA((TOKEN_CHUNKS + 3,)),
        ],
        compiler_params=pltpu.CompilerParams(vmem_limit_bytes=VMEM_LIMIT),
        name="pick_rows",
    )(live_counts, *(in_hbm(array) for array in (ids, gate_vals, tokens, gain)))


def expert_rows(rows, gate_ref, up_ref, down_ref):
    dims = (((1,), (1,)), ((), ()))
    gate_act = lax.dot_general(rows, gate_ref[...], dims, preferred_element_type=jnp.float32)
    up_act = lax.dot_general(rows, up_ref[...], dims, preferred_element_type=jnp.float32)
    hidden = (jax.nn.silu(gate_act) * up_act).astype(jnp.bfloat16)
    partial_out = jnp.dot(hidden, down_ref[...], preferred_element_type=jnp.float32)
    return partial_out.astype(jnp.bfloat16)


def expert_blocks(ins, weights, outs):
    together = max(1, 128 // ins[0].shape[0])
    for first in range(0, len(ins), together):
        some = ins[first : first + together]
        partial_out = expert_rows(jnp.concatenate([ref[...] for ref in some], axis=0), *weights)
        at = 0
        for ref in outs[first : first + together]:
            ref[...] = partial_out[at : at + ref.shape[0]]
            at += ref.shape[0]


def expert_cost(blocks, weights):
    size = sum(weight.size for weight in weights)
    rows = sum(block.shape[0] for block in blocks)
    return pl.CostEstimate(flops=2 * rows * size, bytes_accessed=2 * size, transcendentals=0)


def chunk_copies(source, target, chunks, sems):
    rows = source.shape[0] // chunks
    for i in range(chunks):
        at = pl.ds(i * rows, rows)
        yield pltpu.make_async_copy(source.at[at], target.at[at], sems.at[i])


def stage_kernel(count, *refs):
    *refs, sems = refs
    blocks, sources, out_ref, weights = refs[:count], refs[count : count + 3], refs[-4], refs[-3:]
    copies = [
        copy
        for i, pair in enumerate(zip(sources, weights))
        for copy in chunk_copies(*pair, WEIGHT_CHUNKS, sems.at[i])
    ]
    for copy in copies:
        copy.start()
    at = 0
    for ref in blocks:
        out_ref[at : at + ref.shape[0]] = ref[...]
        at += ref.shape[0]
    for copy in copies:
        copy.wait()


def stage_weights(blocks, weights, after=()):
    vmem = pl.BlockSpec(memory_space=pltpu.VMEM)
    hbm = pl.BlockSpec(memory_space=pltpu.HBM)
    rows = sum(block.shape[0] for block in blocks)
    joined = jax.ShapeDtypeStruct((rows, blocks[0].shape[1]), jnp.bfloat16)
    joined, *weights = pl.pallas_call(
        functools.partial(stage_kernel, len(blocks)),
        out_shape=[joined] + [jax.ShapeDtypeStruct(array.shape, array.dtype) for array in weights],
        in_specs=[vmem] * len(blocks) + [hbm] * 3 + [pl.BlockSpec(memory_space=pl.ANY)] * len(after),
        out_specs=[vmem] * 4,
        scratch_shapes=[pltpu.SemaphoreType.DMA((3, WEIGHT_CHUNKS))],
        compiler_params=pltpu.CompilerParams(vmem_limit_bytes=VMEM_LIMIT),
        cost_estimate=expert_cost(blocks, weights),
        name="stage_weights",
    )(*blocks, *(in_hbm(weight) for weight in weights), *after)
    return joined, weights


def slice_kernel(count, *refs):
    outs = refs[len(refs) - count :]
    expert_blocks(refs[:count], refs[count : count + 3], outs)


def expert_slice(blocks, weights, after=()):
    vmem = pl.BlockSpec(memory_space=pltpu.VMEM)
    count = len(blocks)
    return pl.pallas_call(
        functools.partial(slice_kernel, count),
        out_shape=[jax.ShapeDtypeStruct(block.shape, jnp.bfloat16) for block in blocks],
        in_specs=[vmem] * (count + 3) + [pl.BlockSpec(memory_space=pl.ANY)] * len(after),
        out_specs=[vmem] * count,
        compiler_params=pltpu.CompilerParams(vmem_limit_bytes=VMEM_LIMIT),
        cost_estimate=expert_cost(blocks, weights),
        name="expert_slice",
    )(*blocks, *weights, *after)


def add_level(kept, came):
    return (kept.astype(jnp.float32) + came.astype(jnp.float32)).astype(jnp.bfloat16)


def combine_kernel(table_ref, *refs):
    *parts, out_hbm, out_ref, sems = refs
    table = table_ref[...]
    pieces = []
    for _ in range(3):
        pieces.append(table.astype(jnp.bfloat16))
        table = table - pieces[-1].astype(jnp.float32)
    pieces = jnp.concatenate(pieces, axis=0)
    features = out_ref.shape[1]
    width = features // 4
    copies = []
    for i in range(4):
        columns = pl.ds(i * width, width)
        summed = functools.reduce(add_level, [part[:, columns] for part in parts])
        out_ref[:, columns] = lax.dot_general(
            pieces,
            jnp.concatenate([summed] * 3, axis=0),
            (((0,), (0,)), ((), ())),
            preferred_element_type=jnp.float32,
        ).astype(jnp.bfloat16)
        copies.append(
            pltpu.make_async_copy(out_ref.at[:, columns], out_hbm.at[:, columns], sems.at[i])
        )
        copies[-1].start()
    for copy in copies:
        copy.wait()


def combine(table, parts):
    vmem = pl.BlockSpec(memory_space=pltpu.VMEM)
    shape = (table.shape[1], parts[0].shape[1])
    return pl.pallas_call(
        combine_kernel,
        out_shape=jax.ShapeDtypeStruct(shape, jnp.bfloat16),
        in_specs=[vmem] * (1 + len(parts)),
        out_specs=pl.BlockSpec(memory_space=pltpu.HBM),
        scratch_shapes=[pltpu.VMEM(shape, jnp.bfloat16), pltpu.SemaphoreType.DMA((4,))],
        compiler_params=pltpu.CompilerParams(vmem_limit_bytes=VMEM_LIMIT),
        name="combine",
    )(table, *parts)


def across_groups(flight, blocks):
    if flight == 1:
        return blocks
    groups = [[g * SLICES + m for g in range(flight)] for m in range(SLICES)]
    return lax.all_to_all(
        blocks, "ep", split_axis=0, concat_axis=0, axis_index_groups=groups, tiled=True
    )


def swap(devices, distance, block):
    return lax.ppermute(block, "ep", [(i, i ^ distance) for i in range(devices)])


def on_device(tokens, norm_gain, expert_ids, gate_vals, live_counts, w_gate, w_up, w_down):
    features = tokens.shape[1]
    devices = lax.axis_size("ep")
    flight = devices // SLICES
    slots = flight * CAP
    rows, table = pick_rows(
        slots, live_counts, expert_ids.T, gate_vals.T, tokens, norm_gain.reshape(1, features)
    )
    own = across_groups(flight, rows)
    weights = (w_gate.T, w_up.T, w_down)
    far = swap(devices, 4, own)
    farther = swap(devices, 6, own)
    near = swap(devices, 2, own)
    own_staged, weights = stage_weights((own,), weights, ())
    inner = jnp.concatenate([own, near])
    farther_y, far_y = swap(devices, 1, farther), swap(devices, 1, far)
    inner_y = swap(devices, 1, inner)
    r_farther_y, r_farther = expert_slice((farther_y, farther), weights, ())
    r_far_y, r_far = expert_slice((far_y, far), weights, (near,))
    r_inner_y, r_inner = expert_slice((inner_y, inner), weights, (r_farther_y,))
    c_inner = swap(devices, 1, r_inner_y)
    s_own, s_near = (add_level(r_inner[at], c_inner[at]) for at in (slice(slots), slice(slots, None)))
    w_near = swap(devices, 2, s_near)
    c_outer = swap(devices, 1, jnp.concatenate([r_far_y, r_farther_y]))
    s_far, s_farther = add_level(r_far, c_outer[:slots]), add_level(r_farther, c_outer[slots:])
    w_farther, w_far = swap(devices, 6, s_farther), swap(devices, 4, s_far)
    parts = [s_own, w_near, add_level(w_far, w_farther)]
    if flight > 1:
        parts = [across_groups(flight, functools.reduce(add_level, parts))]
    return combine(table, parts)


def solution(mesh):
    return jax.shard_map(
        on_device,
        mesh=mesh,
        in_specs=(
            P(("sp", "ep"), None),
            P(),
            P(("sp", "ep"), None),
            P(("sp", "ep"), None),
            P(("sp", "ep")),
            P(None, "ep"),
            P(None, "ep"),
            P("ep", None),
        ),
        out_specs=P(("sp", "ep"), None),
        check_vma=False,
    )
```

```python
import functools

import jax
import jax.numpy as jnp
from jax import lax
from jax.experimental import pallas as pl
from jax.experimental.pallas import tpu as pltpu
from jax.sharding import PartitionSpec as P

SLICES = 8
CAP = 16
VMEM_LIMIT = 40 * 1024 * 1024
WEIGHT_CHUNKS = 4
TOKEN_CHUNKS = 4
OUT_CHUNKS = 8


def in_hbm(array):
    return pltpu.with_memory_space_constraint(array, pltpu.HBM)


def pick_kernel(
    live_ref, ids_hbm, gate_hbm, tokens_hbm, gain_hbm, rows_ref, table_ref, ids_ref, gate_ref, tokens_ref, gain_ref, sems
):
    ids_copy, gate_copy, gain_copy = (
        pltpu.make_async_copy(source, target, sems.at[TOKEN_CHUNKS + i])
        for i, (source, target) in enumerate(
            ((ids_hbm, ids_ref), (gate_hbm, gate_ref), (gain_hbm, gain_ref))
        )
    )
    token_copies = list(chunk_copies(tokens_hbm, tokens_ref, TOKEN_CHUNKS, sems))
    for copy in (ids_copy, *token_copies, gain_copy, gate_copy):
        copy.start()
    slots, tok_rows = table_ref.shape
    slot = lax.broadcasted_iota(jnp.int32, (slots, tok_rows), 0)
    token = lax.broadcasted_iota(jnp.int32, (slots, tok_rows), 1)
    expert, place = slot // CAP, slot % CAP
    live = token < live_ref[0]
    before = lax.broadcasted_iota(jnp.int32, (tok_rows, tok_rows), 0)
    after = lax.broadcasted_iota(jnp.int32, (tok_rows, tok_rows), 1)
    earlier = jnp.where(before < after, 1.0, 0.0).astype(jnp.bfloat16)
    ids_copy.wait()
    hits = [(ids_ref[k : k + 1, :] == expert) & live for k in range(ids_ref.shape[0])]
    chosen = jnp.where(functools.reduce(jnp.logical_or, hits), 1.0, 0.0)
    rank = jnp.dot(chosen.astype(jnp.bfloat16), earlier, preferred_element_type=jnp.float32)
    pick = jnp.where((chosen > 0.0) & (rank.astype(jnp.int32) == place), 1.0, 0.0)
    for copy in token_copies:
        copy.wait()
    values = jnp.dot(pick.astype(jnp.bfloat16), tokens_ref[...], preferred_element_type=jnp.float32)
    mean_sq = jnp.mean(values * values, axis=-1, keepdims=True)
    gain_copy.wait()
    rows_ref[...] = (values * lax.rsqrt(mean_sq + 1e-06) * gain_ref[...]).astype(jnp.bfloat16)
    gate_copy.wait()
    weight = jnp.zeros((slots, tok_rows), jnp.float32)
    for k, hit in enumerate(hits):
        weight = jnp.where(hit, gate_ref[k : k + 1, :], weight)
    table_ref[...] = pick * weight


def pick_rows(slots, live_counts, ids, gate_vals, tokens, gain):
    vmem = pl.BlockSpec(memory_space=pltpu.VMEM)
    hbm = pl.BlockSpec(memory_space=pltpu.HBM)
    return pl.pallas_call(
        pick_kernel,
        out_shape=(
            jax.ShapeDtypeStruct((slots, tokens.shape[1]), jnp.bfloat16),
            jax.ShapeDtypeStruct((slots, tokens.shape[0]), jnp.float32),
        ),
        in_specs=[pl.BlockSpec(memory_space=pltpu.SMEM), hbm, hbm, hbm, hbm],
        out_specs=(vmem, vmem),
        scratch_shapes=[
            pltpu.VMEM(ids.shape, ids.dtype),
            pltpu.VMEM(gate_vals.shape, gate_vals.dtype),
            pltpu.VMEM(tokens.shape, tokens.dtype),
            pltpu.VMEM(gain.shape, gain.dtype),
            pltpu.SemaphoreType.DMA((TOKEN_CHUNKS + 3,)),
        ],
        compiler_params=pltpu.CompilerParams(vmem_limit_bytes=VMEM_LIMIT),
        name="pick_rows",
    )(live_counts, *(in_hbm(array) for array in (ids, gate_vals, tokens, gain)))


def expert_rows(rows, gate_ref, up_ref, down_ref):
    dims = (((1,), (1,)), ((), ()))
    gate_act = lax.dot_general(rows, gate_ref[...], dims, preferred_element_type=jnp.float32)
    up_act = lax.dot_general(rows, up_ref[...], dims, preferred_element_type=jnp.float32)
    hidden = (jax.nn.silu(gate_act) * up_act).astype(jnp.bfloat16)
    partial_out = jnp.dot(hidden, down_ref[...], preferred_element_type=jnp.float32)
    return partial_out.astype(jnp.bfloat16)


def expert_blocks(ins, weights, outs):
    size = ins[0].shape[0]
    together = max(1, 128 // size)
    targets = [(ref, at) for ref in outs for at in range(0, ref.shape[0], size)]
    first = 0
    while first < len(ins):
        some = [ref for ref in ins[first : first + together]]
        rows = jnp.concatenate([ref[...] for ref in some], axis=0)
        partial_out = expert_rows(rows, *weights)
        for i, (ref, at) in enumerate(targets[first : first + len(some)]):
            ref[at : at + size] = partial_out[i * size : (i + 1) * size]
        first += together


def expert_cost(blocks, weights):
    size = sum(weight.size for weight in weights)
    rows = sum(block.shape[0] for block in blocks)
    return pl.CostEstimate(flops=2 * rows * size, bytes_accessed=2 * size, transcendentals=0)


def chunk_copies(source, target, chunks, sems):
    rows = source.shape[0] // chunks
    for i in range(chunks):
        at = pl.ds(i * rows, rows)
        yield pltpu.make_async_copy(source.at[at], target.at[at], sems.at[i])


def stage_kernel(*refs):
    *refs, sems = refs
    copies = [
        copy
        for i, pair in enumerate(zip(refs[:3], refs[-3:]))
        for copy in chunk_copies(*pair, WEIGHT_CHUNKS, sems.at[i])
    ]
    for copy in copies:
        copy.start()
    for copy in copies:
        copy.wait()


def stage_weights(weights, after):
    vmem = pl.BlockSpec(memory_space=pltpu.VMEM)
    hbm = pl.BlockSpec(memory_space=pltpu.HBM)
    return pl.pallas_call(
        stage_kernel,
        out_shape=[jax.ShapeDtypeStruct(array.shape, array.dtype) for array in weights],
        in_specs=[hbm] * 3 + [pl.BlockSpec(memory_space=pl.ANY)] * len(after),
        out_specs=[vmem] * 3,
        scratch_shapes=[pltpu.SemaphoreType.DMA((3, WEIGHT_CHUNKS))],
        compiler_params=pltpu.CompilerParams(vmem_limit_bytes=VMEM_LIMIT),
        cost_estimate=expert_cost(after, weights),
        name="stage_weights",
    )(*(in_hbm(weight) for weight in weights), *after)


def slice_kernel(count, made, *refs):
    expert_blocks(refs[:count], refs[count : count + 3], refs[len(refs) - made :])


def expert_slice(groups, weights, after=()):
    vmem = pl.BlockSpec(memory_space=pltpu.VMEM)
    blocks = [block for group in groups for block in group]
    rows, features = blocks[0].shape
    return pl.pallas_call(
        functools.partial(slice_kernel, len(blocks), len(groups)),
        out_shape=[
            jax.ShapeDtypeStruct((rows * len(group), features), jnp.bfloat16) for group in groups
        ],
        in_specs=[vmem] * (len(blocks) + 3) + [pl.BlockSpec(memory_space=pl.ANY)] * len(after),
        out_specs=[vmem] * len(groups),
        compiler_params=pltpu.CompilerParams(vmem_limit_bytes=VMEM_LIMIT),
        cost_estimate=expert_cost(blocks, weights),
        name="expert_slice",
    )(*blocks, *weights, *after)


def add_level(kept, came):
    return (kept.astype(jnp.float32) + came.astype(jnp.float32)).astype(jnp.bfloat16)


def combine_kernel(table_ref, *refs):
    *parts, out_hbm, out_ref, sems = refs
    table = table_ref[...]
    pieces = []
    for _ in range(3):
        pieces.append(table.astype(jnp.bfloat16))
        table = table - pieces[-1].astype(jnp.float32)
    pieces = jnp.concatenate(pieces, axis=0)
    features = out_ref.shape[1]
    width = features // OUT_CHUNKS
    copies = []
    for i in range(OUT_CHUNKS):
        columns = pl.ds(i * width, width)
        summed = functools.reduce(add_level, [part[:, columns] for part in parts])
        out_ref[:, columns] = lax.dot_general(
            pieces,
            jnp.concatenate([summed] * 3, axis=0),
            (((0,), (0,)), ((), ())),
            preferred_element_type=jnp.float32,
        ).astype(jnp.bfloat16)
        copies.append(
            pltpu.make_async_copy(out_ref.at[:, columns], out_hbm.at[:, columns], sems.at[i])
        )
        copies[-1].start()
    for copy in copies:
        copy.wait()


def combine(table, parts):
    vmem = pl.BlockSpec(memory_space=pltpu.VMEM)
    shape = (table.shape[1], parts[0].shape[1])
    return pl.pallas_call(
        combine_kernel,
        out_shape=jax.ShapeDtypeStruct(shape, jnp.bfloat16),
        in_specs=[vmem] * (1 + len(parts)),
        out_specs=pl.BlockSpec(memory_space=pltpu.HBM),
        scratch_shapes=[pltpu.VMEM(shape, jnp.bfloat16), pltpu.SemaphoreType.DMA((OUT_CHUNKS,))],
        compiler_params=pltpu.CompilerParams(vmem_limit_bytes=VMEM_LIMIT),
        name="combine",
    )(table, *parts)


def across_groups(flight, blocks):
    if flight == 1:
        return blocks
    groups = [[g * SLICES + m for g in range(flight)] for m in range(SLICES)]
    return lax.all_to_all(
        blocks, "ep", split_axis=0, concat_axis=0, axis_index_groups=groups, tiled=True
    )


def swap(devices, distance, block):
    return lax.ppermute(block, "ep", [(i, i ^ distance) for i in range(devices)])


def on_device(tokens, norm_gain, expert_ids, gate_vals, live_counts, w_gate, w_up, w_down):
    features = tokens.shape[1]
    devices = lax.axis_size("ep")
    flight = devices // SLICES
    slots = flight * CAP
    rows, table = pick_rows(
        slots, live_counts, expert_ids.T, gate_vals.T, tokens, norm_gain.reshape(1, features)
    )
    own = across_groups(flight, rows)
    far = swap(devices, 4, own)
    near = swap(devices, 2, own)
    farther = swap(devices, 6, own)
    weights = stage_weights((w_gate.T, w_up.T, w_down), (own,))
    inner = jnp.concatenate([own, near])
    farther_y, far_y = swap(devices, 1, farther), swap(devices, 1, far)
    inner_y = swap(devices, 1, inner)
    outer_y, far, farther = expert_slice(((far_y, farther_y), (far,), (farther,)), weights)
    inner_y, inner = expert_slice(((inner_y,), (inner,)), weights, (outer_y,))
    halves = (slice(slots), slice(slots, None))
    outer_c, inner_c = swap(devices, 1, outer_y), swap(devices, 1, inner_y)
    far, farther = (add_level(kept, outer_c[at]) for kept, at in zip((far, farther), halves))
    own, near = (add_level(inner[at], inner_c[at]) for at in halves)
    farther, far = swap(devices, 6, farther), swap(devices, 4, far)
    parts = [own, swap(devices, 2, near), add_level(far, farther)]
    if flight > 1:
        parts = [across_groups(flight, functools.reduce(add_level, parts))]
    return combine(table, parts)


def solution(mesh):
    return jax.shard_map(
        on_device,
        mesh=mesh,
        in_specs=(
            P(("sp", "ep"), None),
            P(),
            P(("sp", "ep"), None),
            P(("sp", "ep"), None),
            P(("sp", "ep")),
            P(None, "ep"),
            P(None, "ep"),
            P("ep", None),
        ),
        out_specs=P(("sp", "ep"), None),
        check_vma=False,
    )
```

```python
import functools

import jax
import jax.numpy as jnp
from jax import lax
from jax.experimental import pallas as pl
from jax.experimental.pallas import tpu as pltpu
from jax.sharding import PartitionSpec as P

SLICES = 8
CAP = 16
VMEM_LIMIT = 40 * 1024 * 1024
WEIGHT_CHUNKS = 4
TOKEN_CHUNKS = 4


def in_hbm(array):
    return pltpu.with_memory_space_constraint(array, pltpu.HBM)


def pick_kernel(
    ids_hbm, gate_hbm, tokens_hbm, gain_hbm, rows_ref, table_ref, ids_ref, gate_ref, tokens_ref, gain_ref, sems
):
    ids_copy, gate_copy, gain_copy = (
        pltpu.make_async_copy(source, target, sems.at[TOKEN_CHUNKS + i])
        for i, (source, target) in enumerate(
            ((ids_hbm, ids_ref), (gate_hbm, gate_ref), (gain_hbm, gain_ref))
        )
    )
    features = tokens_ref.shape[1]
    width = features // TOKEN_CHUNKS
    columns = [pl.ds(i * width, width) for i in range(TOKEN_CHUNKS)]
    token_copies = [
        pltpu.make_async_copy(tokens_hbm.at[:, some], tokens_ref.at[:, some], sems.at[i])
        for i, some in enumerate(columns)
    ]
    for copy in (ids_copy, *token_copies, gain_copy, gate_copy):
        copy.start()
    slots, tok_rows = table_ref.shape
    slot = lax.broadcasted_iota(jnp.int32, (slots, tok_rows), 0)
    expert, place = slot // CAP, slot % CAP
    before = lax.broadcasted_iota(jnp.int32, (tok_rows, tok_rows), 0)
    after = lax.broadcasted_iota(jnp.int32, (tok_rows, tok_rows), 1)
    earlier = jnp.where(before < after, 1.0, 0.0).astype(jnp.bfloat16)
    ids_copy.wait()
    hits = [ids_ref[k : k + 1, :] == expert for k in range(ids_ref.shape[0])]
    chosen = jnp.where(functools.reduce(jnp.logical_or, hits), 1.0, 0.0)
    rank = jnp.dot(chosen.astype(jnp.bfloat16), earlier, preferred_element_type=jnp.float32)
    pick = jnp.where((chosen > 0.0) & (rank.astype(jnp.int32) == place), 1.0, 0.0)
    pick_rows = pick.astype(jnp.bfloat16)
    values, square = [], 0.0
    for copy, some in zip(token_copies, columns):
        copy.wait()
        values.append(jnp.dot(pick_rows, tokens_ref[:, some], preferred_element_type=jnp.float32))
        square = square + jnp.sum(values[-1] * values[-1], axis=-1, keepdims=True)
    scale = lax.rsqrt(square / features + 1e-06)
    gain_copy.wait()
    for part, some in zip(values, columns):
        rows_ref[:, some] = (part * scale * gain_ref[:, some]).astype(jnp.bfloat16)
    gate_copy.wait()
    weight = jnp.zeros((slots, tok_rows), jnp.float32)
    for k, hit in enumerate(hits):
        weight = jnp.where(hit, gate_ref[k : k + 1, :], weight)
    table_ref[...] = pick * weight


def pick_rows(slots, ids, gate_vals, tokens, gain):
    vmem = pl.BlockSpec(memory_space=pltpu.VMEM)
    hbm = pl.BlockSpec(memory_space=pltpu.HBM)
    return pl.pallas_call(
        pick_kernel,
        out_shape=(
            jax.ShapeDtypeStruct((slots, tokens.shape[1]), jnp.bfloat16),
            jax.ShapeDtypeStruct((slots, tokens.shape[0]), jnp.float32),
        ),
        in_specs=[hbm] * 4,
        out_specs=(vmem, vmem),
        scratch_shapes=[
            pltpu.VMEM(ids.shape, ids.dtype),
            pltpu.VMEM(gate_vals.shape, gate_vals.dtype),
            pltpu.VMEM(tokens.shape, tokens.dtype),
            pltpu.VMEM(gain.shape, gain.dtype),
            pltpu.SemaphoreType.DMA((TOKEN_CHUNKS + 3,)),
        ],
        compiler_params=pltpu.CompilerParams(vmem_limit_bytes=VMEM_LIMIT),
        name="pick_rows",
    )(*(in_hbm(array) for array in (ids, gate_vals, tokens, gain)))


def expert_rows(rows, gate_ref, up_ref, down_ref):
    dims = (((1,), (1,)), ((), ()))
    gate_act = lax.dot_general(rows, gate_ref[...], dims, preferred_element_type=jnp.float32)
    up_act = lax.dot_general(rows, up_ref[...], dims, preferred_element_type=jnp.float32)
    hidden = (jax.nn.silu(gate_act) * up_act).astype(jnp.bfloat16)
    partial_out = jnp.dot(hidden, down_ref[...], preferred_element_type=jnp.float32)
    return partial_out.astype(jnp.bfloat16)


def expert_blocks(ins, weights, outs):
    together = max(1, 128 // ins[0].shape[0])
    for first in range(0, len(ins), together):
        some = ins[first : first + together]
        partial_out = expert_rows(jnp.concatenate([ref[...] for ref in some], axis=0), *weights)
        at = 0
        for ref in outs[first : first + together]:
            ref[...] = partial_out[at : at + ref.shape[0]]
            at += ref.shape[0]


def expert_cost(blocks, weights):
    size = sum(weight.size for weight in weights)
    rows = sum(block.shape[0] for block in blocks)
    return pl.CostEstimate(flops=2 * rows * size, bytes_accessed=2 * size, transcendentals=0)


def chunk_copies(source, target, chunks, sems):
    rows = source.shape[0] // chunks
    for i in range(chunks):
        at = pl.ds(i * rows, rows)
        yield pltpu.make_async_copy(source.at[at], target.at[at], sems.at[i])


def stage_kernel(live_ref, rows_ref, table_ref, *refs):
    *refs, sems = refs
    sources, (rows_out, table_out), weights = refs[:3], refs[3:5], refs[5:]
    copies = [
        copy
        for i, pair in enumerate(zip(sources, weights))
        for copy in chunk_copies(*pair, WEIGHT_CHUNKS, sems.at[i])
    ]
    for copy in copies:
        copy.start()
    rows_out[...] = rows_ref[...]
    token = lax.broadcasted_iota(jnp.int32, table_ref.shape, 1)
    table_out[...] = jnp.where(token < live_ref[0], table_ref[...], 0.0)
    for copy in copies:
        copy.wait()


def stage_weights(live_counts, rows, table, weights):
    vmem = pl.BlockSpec(memory_space=pltpu.VMEM)
    hbm = pl.BlockSpec(memory_space=pltpu.HBM)
    arrays = (rows, table, *weights)
    rows, table, *weights = pl.pallas_call(
        stage_kernel,
        out_shape=[jax.ShapeDtypeStruct(array.shape, array.dtype) for array in arrays],
        in_specs=[pl.BlockSpec(memory_space=pltpu.SMEM), vmem, vmem] + [hbm] * 3,
        out_specs=[vmem] * 5,
        scratch_shapes=[pltpu.SemaphoreType.DMA((3, WEIGHT_CHUNKS))],
        compiler_params=pltpu.CompilerParams(vmem_limit_bytes=VMEM_LIMIT),
        cost_estimate=expert_cost([rows], weights),
        name="stage_weights",
    )(live_counts, rows, table, *(in_hbm(weight) for weight in weights))
    return rows, table, weights


def slice_kernel(count, *refs):
    outs = refs[len(refs) - count :]
    expert_blocks(refs[:count], refs[count : count + 3], outs)


def expert_slice(blocks, weights, after=()):
    vmem = pl.BlockSpec(memory_space=pltpu.VMEM)
    count = len(blocks)
    return pl.pallas_call(
        functools.partial(slice_kernel, count),
        out_shape=[jax.ShapeDtypeStruct(block.shape, jnp.bfloat16) for block in blocks],
        in_specs=[vmem] * (count + 3) + [pl.BlockSpec(memory_space=pl.ANY)] * len(after),
        out_specs=[vmem] * count,
        compiler_params=pltpu.CompilerParams(vmem_limit_bytes=VMEM_LIMIT),
        cost_estimate=expert_cost(blocks, weights),
        name="expert_slice",
    )(*blocks, *weights, *after)


def add_level(kept, came):
    return (kept.astype(jnp.float32) + came.astype(jnp.float32)).astype(jnp.bfloat16)


def combine_kernel(table_ref, *refs):
    *parts, out_hbm, out_ref, sems = refs
    table = table_ref[...]
    pieces = []
    for _ in range(3):
        pieces.append(table.astype(jnp.bfloat16))
        table = table - pieces[-1].astype(jnp.float32)
    pieces = jnp.concatenate(pieces, axis=0)
    features = out_ref.shape[1]
    width = features // 4
    copies = []
    for i in range(4):
        columns = pl.ds(i * width, width)
        summed = functools.reduce(add_level, [part[:, columns] for part in parts])
        out_ref[:, columns] = lax.dot_general(
            pieces,
            jnp.concatenate([summed] * 3, axis=0),
            (((0,), (0,)), ((), ())),
            preferred_element_type=jnp.float32,
        ).astype(jnp.bfloat16)
        copies.append(
            pltpu.make_async_copy(out_ref.at[:, columns], out_hbm.at[:, columns], sems.at[i])
        )
        copies[-1].start()
    for copy in copies:
        copy.wait()


def combine(table, parts):
    vmem = pl.BlockSpec(memory_space=pltpu.VMEM)
    shape = (table.shape[1], parts[0].shape[1])
    return pl.pallas_call(
        combine_kernel,
        out_shape=jax.ShapeDtypeStruct(shape, jnp.bfloat16),
        in_specs=[vmem] * (1 + len(parts)),
        out_specs=pl.BlockSpec(memory_space=pltpu.HBM),
        scratch_shapes=[pltpu.VMEM(shape, jnp.bfloat16), pltpu.SemaphoreType.DMA((4,))],
        compiler_params=pltpu.CompilerParams(vmem_limit_bytes=VMEM_LIMIT),
        name="combine",
    )(table, *parts)


def across_groups(flight, blocks):
    if flight == 1:
        return blocks
    groups = [[g * SLICES + m for g in range(flight)] for m in range(SLICES)]
    return lax.all_to_all(
        blocks, "ep", split_axis=0, concat_axis=0, axis_index_groups=groups, tiled=True
    )


def swap(devices, distance, block):
    return lax.ppermute(block, "ep", [(i, i ^ distance) for i in range(devices)])


def on_device(tokens, norm_gain, expert_ids, gate_vals, live_counts, w_gate, w_up, w_down):
    features = tokens.shape[1]
    devices = lax.axis_size("ep")
    flight = devices // SLICES
    slots = flight * CAP
    rows, table = pick_rows(
        slots, expert_ids.T, gate_vals.T, tokens, norm_gain.reshape(1, features)
    )
    own = across_groups(flight, rows)
    farther, far = swap(devices, 6, own), swap(devices, 4, own)
    own, table, weights = stage_weights(live_counts, own, table, (w_gate.T, w_up.T, w_down))
    near = swap(devices, 2, own)
    outer, inner = jnp.concatenate([far, farther]), jnp.concatenate([own, near])
    outer_y, inner_y = swap(devices, 1, outer), swap(devices, 1, inner)
    (outer_y,) = expert_slice((outer_y,), weights)
    outer, inner, inner_y = expert_slice((outer, inner, inner_y), weights, (outer_y,))
    outer_y, inner_y = swap(devices, 1, outer_y), swap(devices, 1, inner_y)
    far, farther = (add_level(outer[at], outer_y[at]) for at in (slice(slots), slice(slots, None)))
    own, near = (add_level(inner[at], inner_y[at]) for at in (slice(slots), slice(slots, None)))
    farther, far = swap(devices, 6, farther), swap(devices, 4, far)
    parts = [own, swap(devices, 2, near), add_level(far, farther)]
    if flight > 1:
        parts = [across_groups(flight, functools.reduce(add_level, parts))]
    return combine(table, parts)


def solution(mesh):
    return jax.shard_map(
        on_device,
        mesh=mesh,
        in_specs=(
            P(("sp", "ep"), None),
            P(),
            P(("sp", "ep"), None),
            P(("sp", "ep"), None),
            P(("sp", "ep")),
            P(None, "ep"),
            P(None, "ep"),
            P("ep", None),
        ),
        out_specs=P(("sp", "ep"), None),
        check_vma=False,
    )
```

```python
import functools

import jax
import jax.numpy as jnp
from jax import lax
from jax.experimental import pallas as pl
from jax.experimental.pallas import tpu as pltpu
from jax.sharding import PartitionSpec as P

SLICES = 8
CAP = 16
VMEM_LIMIT = 40 * 1024 * 1024
WEIGHT_CHUNKS = 4


def in_hbm(array):
    return pltpu.with_memory_space_constraint(array, pltpu.HBM)


def pick_kernel(
    ids_hbm, gate_hbm, tokens_hbm, gain_hbm, rows_ref, table_ref, ids_ref, gate_ref, tokens_ref, gain_ref, sems
):
    ids_copy, gate_copy, gain_copy = (
        pltpu.make_async_copy(source, target, sems.at[i])
        for i, (source, target) in enumerate(
            ((ids_hbm, ids_ref), (gate_hbm, gate_ref), (gain_hbm, gain_ref))
        )
    )
    tokens_copy = pltpu.make_async_copy(tokens_hbm, tokens_ref, sems.at[3])
    for copy in (tokens_copy, ids_copy, gain_copy, gate_copy):
        copy.start()
    slots, tok_rows = table_ref.shape
    slot = lax.broadcasted_iota(jnp.int32, (slots, tok_rows), 0)
    expert, place = slot // CAP, slot % CAP
    before = lax.broadcasted_iota(jnp.int32, (tok_rows, tok_rows), 0)
    after = lax.broadcasted_iota(jnp.int32, (tok_rows, tok_rows), 1)
    earlier = jnp.where(before < after, 1.0, 0.0).astype(jnp.bfloat16)
    ids_copy.wait()
    hits = [ids_ref[k : k + 1, :] == expert for k in range(ids_ref.shape[0])]
    chosen = jnp.where(functools.reduce(jnp.logical_or, hits), 1.0, 0.0)
    rank = jnp.dot(chosen.astype(jnp.bfloat16), earlier, preferred_element_type=jnp.float32)
    pick = jnp.where((chosen > 0.0) & (rank.astype(jnp.int32) == place), 1.0, 0.0)
    tokens_copy.wait()
    values = jnp.dot(pick.astype(jnp.bfloat16), tokens_ref[...], preferred_element_type=jnp.float32)
    mean_sq = jnp.mean(values * values, axis=-1, keepdims=True)
    gain_copy.wait()
    rows_ref[...] = (values * lax.rsqrt(mean_sq + 1e-06) * gain_ref[...]).astype(jnp.bfloat16)
    gate_copy.wait()
    weight = jnp.zeros((slots, tok_rows), jnp.float32)
    for k, hit in enumerate(hits):
        weight = jnp.where(hit, gate_ref[k : k + 1, :], weight)
    table_ref[...] = pick * weight


def pick_rows(slots, ids, gate_vals, tokens, gain):
    vmem = pl.BlockSpec(memory_space=pltpu.VMEM)
    hbm = pl.BlockSpec(memory_space=pltpu.HBM)
    return pl.pallas_call(
        pick_kernel,
        out_shape=(
            jax.ShapeDtypeStruct((slots, tokens.shape[1]), jnp.bfloat16),
            jax.ShapeDtypeStruct((slots, tokens.shape[0]), jnp.float32),
        ),
        in_specs=[hbm] * 4,
        out_specs=(vmem, vmem),
        scratch_shapes=[
            pltpu.VMEM(ids.shape, ids.dtype),
            pltpu.VMEM(gate_vals.shape, gate_vals.dtype),
            pltpu.VMEM(tokens.shape, tokens.dtype),
            pltpu.VMEM(gain.shape, gain.dtype),
            pltpu.SemaphoreType.DMA((4,)),
        ],
        compiler_params=pltpu.CompilerParams(vmem_limit_bytes=VMEM_LIMIT),
        name="pick_rows",
    )(*(in_hbm(array) for array in (ids, gate_vals, tokens, gain)))


def expert_rows(rows, gate_ref, up_ref, down_ref):
    dims = (((1,), (1,)), ((), ()))
    gate_act = lax.dot_general(rows, gate_ref[...], dims, preferred_element_type=jnp.float32)
    up_act = lax.dot_general(rows, up_ref[...], dims, preferred_element_type=jnp.float32)
    hidden = (jax.nn.silu(gate_act) * up_act).astype(jnp.bfloat16)
    partial_out = jnp.dot(hidden, down_ref[...], preferred_element_type=jnp.float32)
    return partial_out.astype(jnp.bfloat16)


def expert_blocks(ins, weights, outs):
    together = max(1, 128 // ins[0].shape[0])
    for first in range(0, len(ins), together):
        some = ins[first : first + together]
        partial_out = expert_rows(jnp.concatenate([ref[...] for ref in some], axis=0), *weights)
        at = 0
        for ref in outs[first : first + together]:
            ref[...] = partial_out[at : at + ref.shape[0]]
            at += ref.shape[0]


def expert_cost(blocks, weights):
    size = sum(weight.size for weight in weights)
    rows = sum(block.shape[0] for block in blocks)
    return pl.CostEstimate(flops=2 * rows * size, bytes_accessed=2 * size, transcendentals=0)


def chunk_copies(source, target, chunks, sems):
    rows = source.shape[0] // chunks
    for i in range(chunks):
        at = pl.ds(i * rows, rows)
        yield pltpu.make_async_copy(source.at[at], target.at[at], sems.at[i])


def stage_kernel(live_ref, rows_ref, table_ref, *refs):
    *refs, sems = refs
    sources, (rows_out, table_out), weights = refs[:3], refs[3:5], refs[5:]
    copies = [
        copy
        for i, pair in enumerate(zip(sources, weights))
        for copy in chunk_copies(*pair, WEIGHT_CHUNKS, sems.at[i])
    ]
    for copy in copies:
        copy.start()
    rows_out[...] = rows_ref[...]
    token = lax.broadcasted_iota(jnp.int32, table_ref.shape, 1)
    table_out[...] = jnp.where(token < live_ref[0], table_ref[...], 0.0)
    for copy in copies:
        copy.wait()


def stage_weights(live_counts, rows, table, weights):
    vmem = pl.BlockSpec(memory_space=pltpu.VMEM)
    hbm = pl.BlockSpec(memory_space=pltpu.HBM)
    arrays = (rows, table, *weights)
    rows, table, *weights = pl.pallas_call(
        stage_kernel,
        out_shape=[jax.ShapeDtypeStruct(array.shape, array.dtype) for array in arrays],
        in_specs=[pl.BlockSpec(memory_space=pltpu.SMEM), vmem, vmem] + [hbm] * 3,
        out_specs=[vmem] * 5,
        scratch_shapes=[pltpu.SemaphoreType.DMA((3, WEIGHT_CHUNKS))],
        compiler_params=pltpu.CompilerParams(vmem_limit_bytes=VMEM_LIMIT),
        cost_estimate=expert_cost([rows], weights),
        name="stage_weights",
    )(live_counts, rows, table, *(in_hbm(weight) for weight in weights))
    return rows, table, weights


def slice_kernel(count, *refs):
    outs = refs[len(refs) - count :]
    expert_blocks(refs[:count], refs[count : count + 3], outs)


def expert_slice(blocks, weights, after=()):
    vmem = pl.BlockSpec(memory_space=pltpu.VMEM)
    count = len(blocks)
    return pl.pallas_call(
        functools.partial(slice_kernel, count),
        out_shape=[jax.ShapeDtypeStruct(block.shape, jnp.bfloat16) for block in blocks],
        in_specs=[vmem] * (count + 3) + [pl.BlockSpec(memory_space=pl.ANY)] * len(after),
        out_specs=[vmem] * count,
        compiler_params=pltpu.CompilerParams(vmem_limit_bytes=VMEM_LIMIT),
        cost_estimate=expert_cost(blocks, weights),
        name="expert_slice",
    )(*blocks, *weights, *after)


def add_level(kept, came):
    return (kept.astype(jnp.float32) + came.astype(jnp.float32)).astype(jnp.bfloat16)


def combine_kernel(table_ref, *refs):
    *parts, out_hbm, out_ref, sems = refs
    table = table_ref[...]
    pieces = []
    for _ in range(3):
        pieces.append(table.astype(jnp.bfloat16))
        table = table - pieces[-1].astype(jnp.float32)
    pieces = jnp.concatenate(pieces, axis=0)
    features = out_ref.shape[1]
    width = features // 4
    copies = []
    for i in range(4):
        columns = pl.ds(i * width, width)
        summed = functools.reduce(add_level, [part[:, columns] for part in parts])
        out_ref[:, columns] = lax.dot_general(
            pieces,
            jnp.concatenate([summed] * 3, axis=0),
            (((0,), (0,)), ((), ())),
            preferred_element_type=jnp.float32,
        ).astype(jnp.bfloat16)
        copies.append(
            pltpu.make_async_copy(out_ref.at[:, columns], out_hbm.at[:, columns], sems.at[i])
        )
        copies[-1].start()
    for copy in copies:
        copy.wait()


def combine(table, parts):
    vmem = pl.BlockSpec(memory_space=pltpu.VMEM)
    shape = (table.shape[1], parts[0].shape[1])
    return pl.pallas_call(
        combine_kernel,
        out_shape=jax.ShapeDtypeStruct(shape, jnp.bfloat16),
        in_specs=[vmem] * (1 + len(parts)),
        out_specs=pl.BlockSpec(memory_space=pltpu.HBM),
        scratch_shapes=[pltpu.VMEM(shape, jnp.bfloat16), pltpu.SemaphoreType.DMA((4,))],
        compiler_params=pltpu.CompilerParams(vmem_limit_bytes=VMEM_LIMIT),
        name="combine",
    )(table, *parts)


def across_groups(flight, blocks):
    if flight == 1:
        return blocks
    groups = [[g * SLICES + m for g in range(flight)] for m in range(SLICES)]
    return lax.all_to_all(
        blocks, "ep", split_axis=0, concat_axis=0, axis_index_groups=groups, tiled=True
    )


def swap(devices, distance, block):
    return lax.ppermute(block, "ep", [(i, i ^ distance) for i in range(devices)])


def on_device(tokens, norm_gain, expert_ids, gate_vals, live_counts, w_gate, w_up, w_down):
    features = tokens.shape[1]
    devices = lax.axis_size("ep")
    flight = devices // SLICES
    slots = flight * CAP
    rows, table = pick_rows(
        slots, expert_ids.T, gate_vals.T, tokens, norm_gain.reshape(1, features)
    )
    own = across_groups(flight, rows)
    farther, far = swap(devices, 6, own), swap(devices, 4, own)
    own, table, weights = stage_weights(live_counts, own, table, (w_gate.T, w_up.T, w_down))
    near = swap(devices, 2, own)
    outer, inner = jnp.concatenate([far, farther]), jnp.concatenate([own, near])
    outer_y, inner_y = swap(devices, 1, outer), swap(devices, 1, inner)
    (outer_y,) = expert_slice((outer_y,), weights)
    outer, inner, inner_y = expert_slice((outer, inner, inner_y), weights, (outer_y,))
    outer_y, inner_y = swap(devices, 1, outer_y), swap(devices, 1, inner_y)
    far, farther = (add_level(outer[at], outer_y[at]) for at in (slice(slots), slice(slots, None)))
    own, near = (add_level(inner[at], inner_y[at]) for at in (slice(slots), slice(slots, None)))
    farther, far = swap(devices, 6, farther), swap(devices, 4, far)
    parts = [own, swap(devices, 2, near), add_level(far, farther)]
    if flight > 1:
        parts = [across_groups(flight, functools.reduce(add_level, parts))]
    return combine(table, parts)


def solution(mesh):
    return jax.shard_map(
        on_device,
        mesh=mesh,
        in_specs=(
            P(("sp", "ep"), None),
            P(),
            P(("sp", "ep"), None),
            P(("sp", "ep"), None),
            P(("sp", "ep")),
            P(None, "ep"),
            P(None, "ep"),
            P("ep", None),
        ),
        out_specs=P(("sp", "ep"), None),
        check_vma=False,
    )
```

```python
import functools

import jax
import jax.numpy as jnp
from jax import lax
from jax.experimental import pallas as pl
from jax.experimental.pallas import tpu as pltpu
from jax.sharding import PartitionSpec as P

SLICES = 8
CAP = 16
VMEM_LIMIT = 40 * 1024 * 1024
WEIGHT_CHUNKS = 4


def in_hbm(array):
    return pltpu.with_memory_space_constraint(array, pltpu.HBM)


def pick_kernel(
    ids_hbm, gate_hbm, tokens_hbm, gain_hbm, rows_ref, table_ref, ids_ref, gate_ref, tokens_ref, gain_ref, sems
):
    ids_copy, gate_copy, gain_copy = (
        pltpu.make_async_copy(source, target, sems.at[i])
        for i, (source, target) in enumerate(
            ((ids_hbm, ids_ref), (gate_hbm, gate_ref), (gain_hbm, gain_ref))
        )
    )
    tokens_copy = pltpu.make_async_copy(tokens_hbm, tokens_ref, sems.at[3])
    for copy in (tokens_copy, ids_copy, gain_copy, gate_copy):
        copy.start()
    slots, tok_rows = table_ref.shape
    slot = lax.broadcasted_iota(jnp.int32, (slots, tok_rows), 0)
    expert, place = slot // CAP, slot % CAP
    before = lax.broadcasted_iota(jnp.int32, (tok_rows, tok_rows), 0)
    after = lax.broadcasted_iota(jnp.int32, (tok_rows, tok_rows), 1)
    earlier = jnp.where(before < after, 1.0, 0.0).astype(jnp.bfloat16)
    ids_copy.wait()
    hits = [ids_ref[k : k + 1, :] == expert for k in range(ids_ref.shape[0])]
    chosen = jnp.where(functools.reduce(jnp.logical_or, hits), 1.0, 0.0)
    rank = jnp.dot(chosen.astype(jnp.bfloat16), earlier, preferred_element_type=jnp.float32)
    pick = jnp.where((chosen > 0.0) & (rank.astype(jnp.int32) == place), 1.0, 0.0)
    tokens_copy.wait()
    values = jnp.dot(pick.astype(jnp.bfloat16), tokens_ref[...], preferred_element_type=jnp.float32)
    mean_sq = jnp.mean(values * values, axis=-1, keepdims=True)
    gain_copy.wait()
    rows_ref[...] = (values * lax.rsqrt(mean_sq + 1e-06) * gain_ref[...]).astype(jnp.bfloat16)
    gate_copy.wait()
    weight = jnp.zeros((slots, tok_rows), jnp.float32)
    for k, hit in enumerate(hits):
        weight = jnp.where(hit, gate_ref[k : k + 1, :], weight)
    table_ref[...] = pick * weight


def pick_rows(slots, ids, gate_vals, tokens, gain):
    vmem = pl.BlockSpec(memory_space=pltpu.VMEM)
    hbm = pl.BlockSpec(memory_space=pltpu.HBM)
    return pl.pallas_call(
        pick_kernel,
        out_shape=(
            jax.ShapeDtypeStruct((slots, tokens.shape[1]), jnp.bfloat16),
            jax.ShapeDtypeStruct((slots, tokens.shape[0]), jnp.float32),
        ),
        in_specs=[hbm] * 4,
        out_specs=(vmem, vmem),
        scratch_shapes=[
            pltpu.VMEM(ids.shape, ids.dtype),
            pltpu.VMEM(gate_vals.shape, gate_vals.dtype),
            pltpu.VMEM(tokens.shape, tokens.dtype),
            pltpu.VMEM(gain.shape, gain.dtype),
            pltpu.SemaphoreType.DMA((4,)),
        ],
        compiler_params=pltpu.CompilerParams(vmem_limit_bytes=VMEM_LIMIT),
        name="pick_rows",
    )(*(in_hbm(array) for array in (ids, gate_vals, tokens, gain)))


def expert_rows(rows, gate_ref, up_ref, down_ref):
    dims = (((1,), (1,)), ((), ()))
    gate_act = lax.dot_general(rows, gate_ref[...], dims, preferred_element_type=jnp.float32)
    up_act = lax.dot_general(rows, up_ref[...], dims, preferred_element_type=jnp.float32)
    hidden = (jax.nn.silu(gate_act) * up_act).astype(jnp.bfloat16)
    partial_out = jnp.dot(hidden, down_ref[...], preferred_element_type=jnp.float32)
    return partial_out.astype(jnp.bfloat16)


def expert_blocks(ins, weights, outs):
    together = max(1, 128 // ins[0].shape[0])
    for first in range(0, len(ins), together):
        some = ins[first : first + together]
        partial_out = expert_rows(jnp.concatenate([ref[...] for ref in some], axis=0), *weights)
        at = 0
        for ref in outs[first : first + together]:
            ref[...] = partial_out[at : at + ref.shape[0]]
            at += ref.shape[0]


def expert_cost(blocks, weights):
    size = sum(weight.size for weight in weights)
    rows = sum(block.shape[0] for block in blocks)
    return pl.CostEstimate(flops=2 * rows * size, bytes_accessed=2 * size, transcendentals=0)


def chunk_copies(source, target, chunks, sems):
    rows = source.shape[0] // chunks
    for i in range(chunks):
        at = pl.ds(i * rows, rows)
        yield pltpu.make_async_copy(source.at[at], target.at[at], sems.at[i])


def stage_kernel(live_ref, rows_ref, table_ref, *refs):
    *refs, sems = refs
    sources, (rows_out, table_out), weights = refs[:3], refs[3:5], refs[5:]
    copies = [
        copy
        for i, pair in enumerate(zip(sources, weights))
        for copy in chunk_copies(*pair, WEIGHT_CHUNKS, sems.at[i])
    ]
    for copy in copies:
        copy.start()
    rows_out[...] = rows_ref[...]
    token = lax.broadcasted_iota(jnp.int32, table_ref.shape, 1)
    table = jnp.where(token < live_ref[0], table_ref[...], 0.0)
    pieces = []
    for _ in range(3):
        pieces.append(table.astype(jnp.bfloat16).astype(jnp.float32))
        table = table - pieces[-1]
    table_out[...] = jnp.concatenate(pieces, axis=0).T.astype(jnp.bfloat16)
    for copy in copies:
        copy.wait()


def stage_weights(live_counts, rows, table, weights):
    vmem = pl.BlockSpec(memory_space=pltpu.VMEM)
    hbm = pl.BlockSpec(memory_space=pltpu.HBM)
    table_shape = (table.shape[1], 3 * table.shape[0])
    rows, table, *weights = pl.pallas_call(
        stage_kernel,
        out_shape=[
            jax.ShapeDtypeStruct(shape, jnp.bfloat16)
            for shape in (rows.shape, table_shape, *(weight.shape for weight in weights))
        ],
        in_specs=[pl.BlockSpec(memory_space=pltpu.SMEM), vmem, vmem] + [hbm] * 3,
        out_specs=[vmem] * 5,
        scratch_shapes=[pltpu.SemaphoreType.DMA((3, WEIGHT_CHUNKS))],
        compiler_params=pltpu.CompilerParams(vmem_limit_bytes=VMEM_LIMIT),
        cost_estimate=expert_cost([rows], weights),
        name="stage_weights",
    )(live_counts, rows, table, *(in_hbm(weight) for weight in weights))
    return rows, table, weights


def slice_kernel(count, *refs):
    outs = refs[len(refs) - count :]
    expert_blocks(refs[:count], refs[count : count + 3], outs)


def expert_slice(blocks, weights, after=()):
    vmem = pl.BlockSpec(memory_space=pltpu.VMEM)
    count = len(blocks)
    return pl.pallas_call(
        functools.partial(slice_kernel, count),
        out_shape=[jax.ShapeDtypeStruct(block.shape, jnp.bfloat16) for block in blocks],
        in_specs=[vmem] * (count + 3) + [pl.BlockSpec(memory_space=pl.ANY)] * len(after),
        out_specs=[vmem] * count,
        compiler_params=pltpu.CompilerParams(vmem_limit_bytes=VMEM_LIMIT),
        cost_estimate=expert_cost(blocks, weights),
        name="expert_slice",
    )(*blocks, *weights, *after)


def add_level(kept, came):
    return (kept.astype(jnp.float32) + came.astype(jnp.float32)).astype(jnp.bfloat16)


def combine_kernel(table_ref, *refs):
    *parts, out_hbm, out_ref, sems = refs
    features = out_ref.shape[1]
    width = features // 4
    copies = []
    for i in range(4):
        columns = pl.ds(i * width, width)
        summed = functools.reduce(add_level, [part[:, columns] for part in parts])
        result = jnp.dot(
            table_ref[...],
            jnp.concatenate([summed] * 3, axis=0),
            preferred_element_type=jnp.float32,
        )
        out_ref[:, columns] = result.astype(jnp.bfloat16)
        copies.append(
            pltpu.make_async_copy(out_ref.at[:, columns], out_hbm.at[:, columns], sems.at[i])
        )
        copies[-1].start()
    for copy in copies:
        copy.wait()


def combine(table, parts):
    vmem = pl.BlockSpec(memory_space=pltpu.VMEM)
    shape = (table.shape[0], parts[0].shape[1])
    return pl.pallas_call(
        combine_kernel,
        out_shape=jax.ShapeDtypeStruct(shape, jnp.bfloat16),
        in_specs=[vmem] * (1 + len(parts)),
        out_specs=pl.BlockSpec(memory_space=pltpu.HBM),
        scratch_shapes=[pltpu.VMEM(shape, jnp.bfloat16), pltpu.SemaphoreType.DMA((4,))],
        compiler_params=pltpu.CompilerParams(vmem_limit_bytes=VMEM_LIMIT),
        name="combine",
    )(table, *parts)


def across_groups(flight, blocks):
    if flight == 1:
        return blocks
    groups = [[g * SLICES + m for g in range(flight)] for m in range(SLICES)]
    return lax.all_to_all(
        blocks, "ep", split_axis=0, concat_axis=0, axis_index_groups=groups, tiled=True
    )


def swap(devices, distance, block):
    return lax.ppermute(block, "ep", [(i, i ^ distance) for i in range(devices)])


def on_device(tokens, norm_gain, expert_ids, gate_vals, live_counts, w_gate, w_up, w_down):
    features = tokens.shape[1]
    devices = lax.axis_size("ep")
    flight = devices // SLICES
    slots = flight * CAP
    rows, table = pick_rows(
        slots, expert_ids.T, gate_vals.T, tokens, norm_gain.reshape(1, features)
    )
    own = across_groups(flight, rows)
    farther, far = swap(devices, 6, own), swap(devices, 4, own)
    own, table, weights = stage_weights(live_counts, own, table, (w_gate.T, w_up.T, w_down))
    near = swap(devices, 2, own)
    outer, inner = jnp.concatenate([far, farther]), jnp.concatenate([own, near])
    outer_y, inner_y = swap(devices, 1, outer), swap(devices, 1, inner)
    (outer_y,) = expert_slice((outer_y,), weights)
    outer, inner, inner_y = expert_slice((outer, inner, inner_y), weights, (outer_y,))
    outer_y, inner_y = swap(devices, 1, outer_y), swap(devices, 1, inner_y)
    far, farther = (add_level(outer[at], outer_y[at]) for at in (slice(slots), slice(slots, None)))
    own, near = (add_level(inner[at], inner_y[at]) for at in (slice(slots), slice(slots, None)))
    farther, far = swap(devices, 6, farther), swap(devices, 4, far)
    parts = [own, swap(devices, 2, near), add_level(far, farther)]
    if flight > 1:
        parts = [across_groups(flight, functools.reduce(add_level, parts))]
    return combine(table, parts)


def solution(mesh):
    return jax.shard_map(
        on_device,
        mesh=mesh,
        in_specs=(
            P(("sp", "ep"), None),
            P(),
            P(("sp", "ep"), None),
            P(("sp", "ep"), None),
            P(("sp", "ep")),
            P(None, "ep"),
            P(None, "ep"),
            P("ep", None),
        ),
        out_specs=P(("sp", "ep"), None),
        check_vma=False,
    )
```

```python
import functools

import jax
import jax.numpy as jnp
from jax import lax
from jax.experimental import pallas as pl
from jax.experimental.pallas import tpu as pltpu
from jax.sharding import PartitionSpec as P

SLICES = 8
CAP = 16
VMEM_LIMIT = 40 * 1024 * 1024
WEIGHT_CHUNKS = 4


def in_hbm(array):
    return pltpu.with_memory_space_constraint(array, pltpu.HBM)


def pick_kernel(
    ids_hbm, gate_hbm, tokens_hbm, gain_hbm, rows_ref, table_ref, ids_ref, gate_ref, tokens_ref, gain_ref, sems
):
    ids_copy, gate_copy, gain_copy = (
        pltpu.make_async_copy(source, target, sems.at[i])
        for i, (source, target) in enumerate(
            ((ids_hbm, ids_ref), (gate_hbm, gate_ref), (gain_hbm, gain_ref))
        )
    )
    tokens_copy = pltpu.make_async_copy(tokens_hbm, tokens_ref, sems.at[3])
    for copy in (tokens_copy, ids_copy, gain_copy, gate_copy):
        copy.start()
    slots, tok_rows = table_ref.shape
    slot = lax.broadcasted_iota(jnp.int32, (slots, tok_rows), 0)
    expert, place = slot // CAP, slot % CAP
    before = lax.broadcasted_iota(jnp.int32, (tok_rows, tok_rows), 0)
    after = lax.broadcasted_iota(jnp.int32, (tok_rows, tok_rows), 1)
    earlier = jnp.where(before < after, 1.0, 0.0).astype(jnp.bfloat16)
    ids_copy.wait()
    hits = [ids_ref[k : k + 1, :] == expert for k in range(ids_ref.shape[0])]
    chosen = jnp.where(functools.reduce(jnp.logical_or, hits), 1.0, 0.0)
    rank = jnp.dot(chosen.astype(jnp.bfloat16), earlier, preferred_element_type=jnp.float32)
    pick = jnp.where((chosen > 0.0) & (rank.astype(jnp.int32) == place), 1.0, 0.0)
    tokens_copy.wait()
    values = jnp.dot(pick.astype(jnp.bfloat16), tokens_ref[...], preferred_element_type=jnp.float32)
    mean_sq = jnp.mean(values * values, axis=-1, keepdims=True)
    gain_copy.wait()
    rows_ref[...] = (values * lax.rsqrt(mean_sq + 1e-06) * gain_ref[...]).astype(jnp.bfloat16)
    gate_copy.wait()
    weight = jnp.zeros((slots, tok_rows), jnp.float32)
    for k, hit in enumerate(hits):
        weight = jnp.where(hit, gate_ref[k : k + 1, :], weight)
    table_ref[...] = pick * weight


def pick_rows(slots, ids, gate_vals, tokens, gain):
    vmem = pl.BlockSpec(memory_space=pltpu.VMEM)
    hbm = pl.BlockSpec(memory_space=pltpu.HBM)
    return pl.pallas_call(
        pick_kernel,
        out_shape=(
            jax.ShapeDtypeStruct((slots, tokens.shape[1]), jnp.bfloat16),
            jax.ShapeDtypeStruct((slots, tokens.shape[0]), jnp.float32),
        ),
        in_specs=[hbm] * 4,
        out_specs=(vmem, vmem),
        scratch_shapes=[
            pltpu.VMEM(ids.shape, ids.dtype),
            pltpu.VMEM(gate_vals.shape, gate_vals.dtype),
            pltpu.VMEM(tokens.shape, tokens.dtype),
            pltpu.VMEM(gain.shape, gain.dtype),
            pltpu.SemaphoreType.DMA((4,)),
        ],
        compiler_params=pltpu.CompilerParams(vmem_limit_bytes=VMEM_LIMIT),
        name="pick_rows",
    )(*(in_hbm(array) for array in (ids, gate_vals, tokens, gain)))


def expert_rows(rows, gate_ref, up_ref, down_ref):
    across, down = (((1,), (1,)), ((), ())), (((0,), (0,)), ((), ()))
    gate_act = lax.dot_general(gate_ref[...], rows, across, preferred_element_type=jnp.float32)
    up_act = lax.dot_general(up_ref[...], rows, across, preferred_element_type=jnp.float32)
    hidden = (jax.nn.silu(gate_act) * up_act).astype(jnp.bfloat16)
    partial_out = lax.dot_general(hidden, down_ref[...], down, preferred_element_type=jnp.float32)
    return partial_out.astype(jnp.bfloat16)


def expert_blocks(ins, weights, outs):
    together = max(1, 128 // ins[0].shape[0])
    for first in range(0, len(ins), together):
        some = ins[first : first + together]
        partial_out = expert_rows(jnp.concatenate([ref[...] for ref in some], axis=0), *weights)
        at = 0
        for ref in outs[first : first + together]:
            ref[...] = partial_out[at : at + ref.shape[0]]
            at += ref.shape[0]


def expert_cost(blocks, weights):
    size = sum(weight.size for weight in weights)
    rows = sum(block.shape[0] for block in blocks)
    return pl.CostEstimate(flops=2 * rows * size, bytes_accessed=2 * size, transcendentals=0)


def chunk_copies(source, target, chunks, sems):
    rows = source.shape[0] // chunks
    for i in range(chunks):
        at = pl.ds(i * rows, rows)
        yield pltpu.make_async_copy(source.at[at], target.at[at], sems.at[i])


def stage_kernel(live_ref, rows_ref, table_ref, *refs):
    *refs, sems = refs
    sources, (rows_out, table_out), weights = refs[:3], refs[3:5], refs[5:]
    copies = [
        copy
        for i, pair in enumerate(zip(sources, weights))
        for copy in chunk_copies(*pair, WEIGHT_CHUNKS, sems.at[i])
    ]
    for copy in copies:
        copy.start()
    rows_out[...] = rows_ref[...]
    token = lax.broadcasted_iota(jnp.int32, table_ref.shape, 1)
    table = jnp.where(token < live_ref[0], table_ref[...], 0.0)
    pieces = []
    for _ in range(3):
        pieces.append(table.astype(jnp.bfloat16).astype(jnp.float32))
        table = table - pieces[-1]
    table_out[...] = jnp.concatenate(pieces, axis=0).T.astype(jnp.bfloat16)
    for copy in copies:
        copy.wait()


def stage_weights(live_counts, rows, table, weights):
    vmem = pl.BlockSpec(memory_space=pltpu.VMEM)
    hbm = pl.BlockSpec(memory_space=pltpu.HBM)
    table_shape = (table.shape[1], 3 * table.shape[0])
    rows, table, *weights = pl.pallas_call(
        stage_kernel,
        out_shape=[
            jax.ShapeDtypeStruct(shape, jnp.bfloat16)
            for shape in (rows.shape, table_shape, *(weight.shape for weight in weights))
        ],
        in_specs=[pl.BlockSpec(memory_space=pltpu.SMEM), vmem, vmem] + [hbm] * 3,
        out_specs=[vmem] * 5,
        scratch_shapes=[pltpu.SemaphoreType.DMA((3, WEIGHT_CHUNKS))],
        compiler_params=pltpu.CompilerParams(vmem_limit_bytes=VMEM_LIMIT),
        cost_estimate=expert_cost([rows], weights),
        name="stage_weights",
    )(live_counts, rows, table, *(in_hbm(weight) for weight in weights))
    return rows, table, weights


def slice_kernel(count, *refs):
    outs = refs[len(refs) - count :]
    expert_blocks(refs[:count], refs[count : count + 3], outs)


def expert_slice(blocks, weights, after=()):
    vmem = pl.BlockSpec(memory_space=pltpu.VMEM)
    count = len(blocks)
    return pl.pallas_call(
        functools.partial(slice_kernel, count),
        out_shape=[jax.ShapeDtypeStruct(block.shape, jnp.bfloat16) for block in blocks],
        in_specs=[vmem] * (count + 3) + [pl.BlockSpec(memory_space=pl.ANY)] * len(after),
        out_specs=[vmem] * count,
        compiler_params=pltpu.CompilerParams(vmem_limit_bytes=VMEM_LIMIT),
        cost_estimate=expert_cost(blocks, weights),
        name="expert_slice",
    )(*blocks, *weights, *after)


def add_level(kept, came):
    return (kept.astype(jnp.float32) + came.astype(jnp.float32)).astype(jnp.bfloat16)


def combine_kernel(table_ref, *refs):
    *parts, out_hbm, out_ref, sems = refs
    features = out_ref.shape[1]
    width = features // 4
    copies = []
    for i in range(4):
        columns = pl.ds(i * width, width)
        summed = functools.reduce(add_level, [part[:, columns] for part in parts])
        result = jnp.dot(
            table_ref[...],
            jnp.concatenate([summed] * 3, axis=0),
            preferred_element_type=jnp.float32,
        )
        out_ref[:, columns] = result.astype(jnp.bfloat16)
        copies.append(
            pltpu.make_async_copy(out_ref.at[:, columns], out_hbm.at[:, columns], sems.at[i])
        )
        copies[-1].start()
    for copy in copies:
        copy.wait()


def combine(table, parts):
    vmem = pl.BlockSpec(memory_space=pltpu.VMEM)
    shape = (table.shape[0], parts[0].shape[1])
    return pl.pallas_call(
        combine_kernel,
        out_shape=jax.ShapeDtypeStruct(shape, jnp.bfloat16),
        in_specs=[vmem] * (1 + len(parts)),
        out_specs=pl.BlockSpec(memory_space=pltpu.HBM),
        scratch_shapes=[pltpu.VMEM(shape, jnp.bfloat16), pltpu.SemaphoreType.DMA((4,))],
        compiler_params=pltpu.CompilerParams(vmem_limit_bytes=VMEM_LIMIT),
        name="combine",
    )(table, *parts)


def across_groups(flight, blocks):
    if flight == 1:
        return blocks
    groups = [[g * SLICES + m for g in range(flight)] for m in range(SLICES)]
    return lax.all_to_all(
        blocks, "ep", split_axis=0, concat_axis=0, axis_index_groups=groups, tiled=True
    )


def swap(devices, distance, block):
    return lax.ppermute(block, "ep", [(i, i ^ distance) for i in range(devices)])


def on_device(tokens, norm_gain, expert_ids, gate_vals, live_counts, w_gate, w_up, w_down):
    features = tokens.shape[1]
    devices = lax.axis_size("ep")
    flight = devices // SLICES
    slots = flight * CAP
    rows, table = pick_rows(
        slots, expert_ids.T, gate_vals.T, tokens, norm_gain.reshape(1, features)
    )
    own = across_groups(flight, rows)
    farther, far = swap(devices, 6, own), swap(devices, 4, own)
    own, table, weights = stage_weights(live_counts, own, table, (w_gate.T, w_up.T, w_down))
    near = swap(devices, 2, own)
    outer, inner = jnp.concatenate([far, farther]), jnp.concatenate([own, near])
    outer_y, inner_y = swap(devices, 1, outer), swap(devices, 1, inner)
    (outer_y,) = expert_slice((outer_y,), weights)
    outer, inner, inner_y = expert_slice((outer, inner, inner_y), weights, (outer_y,))
    outer_y, inner_y = swap(devices, 1, outer_y), swap(devices, 1, inner_y)
    far, farther = (add_level(outer[at], outer_y[at]) for at in (slice(slots), slice(slots, None)))
    own, near = (add_level(inner[at], inner_y[at]) for at in (slice(slots), slice(slots, None)))
    farther, far = swap(devices, 6, farther), swap(devices, 4, far)
    parts = [own, swap(devices, 2, near), add_level(far, farther)]
    if flight > 1:
        parts = [across_groups(flight, functools.reduce(add_level, parts))]
    return combine(table, parts)


def solution(mesh):
    return jax.shard_map(
        on_device,
        mesh=mesh,
        in_specs=(
            P(("sp", "ep"), None),
            P(),
            P(("sp", "ep"), None),
            P(("sp", "ep"), None),
            P(("sp", "ep")),
            P(None, "ep"),
            P(None, "ep"),
            P("ep", None),
        ),
        out_specs=P(("sp", "ep"), None),
        check_vma=False,
    )
```

```python
import functools

import jax
import jax.numpy as jnp
from jax import lax
from jax.experimental import pallas as pl
from jax.experimental.pallas import tpu as pltpu
from jax.sharding import PartitionSpec as P

SLICES = 8
CAP = 16
VMEM_LIMIT = 40 * 1024 * 1024
WEIGHT_CHUNKS = 4


def in_hbm(array):
    return pltpu.with_memory_space_constraint(array, pltpu.HBM)


def pick_kernel(
    ids_hbm, gate_hbm, tokens_hbm, gain_hbm, rows_ref, table_ref, ids_ref, gate_ref, tokens_ref, gain_ref, sems
):
    ids_copy, gate_copy, gain_copy = (
        pltpu.make_async_copy(source, target, sems.at[i])
        for i, (source, target) in enumerate(
            ((ids_hbm, ids_ref), (gate_hbm, gate_ref), (gain_hbm, gain_ref))
        )
    )
    tokens_copy = pltpu.make_async_copy(tokens_hbm, tokens_ref, sems.at[3])
    for copy in (tokens_copy, ids_copy, gain_copy, gate_copy):
        copy.start()
    slots, tok_rows = table_ref.shape
    slot = lax.broadcasted_iota(jnp.int32, (slots, tok_rows), 0)
    expert, place = slot // CAP, slot % CAP
    before = lax.broadcasted_iota(jnp.int32, (tok_rows, tok_rows), 0)
    after = lax.broadcasted_iota(jnp.int32, (tok_rows, tok_rows), 1)
    earlier = jnp.where(before < after, 1.0, 0.0).astype(jnp.bfloat16)
    ids_copy.wait()
    hits = [ids_ref[k : k + 1, :] == expert for k in range(ids_ref.shape[0])]
    chosen = jnp.where(functools.reduce(jnp.logical_or, hits), 1.0, 0.0)
    rank = jnp.dot(chosen.astype(jnp.bfloat16), earlier, preferred_element_type=jnp.float32)
    pick = jnp.where((chosen > 0.0) & (rank.astype(jnp.int32) == place), 1.0, 0.0)
    tokens_copy.wait()
    values = jnp.dot(pick.astype(jnp.bfloat16), tokens_ref[...], preferred_element_type=jnp.float32)
    mean_sq = jnp.mean(values * values, axis=-1, keepdims=True)
    gain_copy.wait()
    rows_ref[...] = (values * lax.rsqrt(mean_sq + 1e-06) * gain_ref[...]).astype(jnp.bfloat16)
    gate_copy.wait()
    weight = jnp.zeros((slots, tok_rows), jnp.float32)
    for k, hit in enumerate(hits):
        weight = jnp.where(hit, gate_ref[k : k + 1, :], weight)
    table_ref[...] = pick * weight


def pick_rows(slots, ids, gate_vals, tokens, gain):
    vmem = pl.BlockSpec(memory_space=pltpu.VMEM)
    hbm = pl.BlockSpec(memory_space=pltpu.HBM)
    return pl.pallas_call(
        pick_kernel,
        out_shape=(
            jax.ShapeDtypeStruct((slots, tokens.shape[1]), jnp.bfloat16),
            jax.ShapeDtypeStruct((slots, tokens.shape[0]), jnp.float32),
        ),
        in_specs=[hbm] * 4,
        out_specs=(vmem, vmem),
        scratch_shapes=[
            pltpu.VMEM(ids.shape, ids.dtype),
            pltpu.VMEM(gate_vals.shape, gate_vals.dtype),
            pltpu.VMEM(tokens.shape, tokens.dtype),
            pltpu.VMEM(gain.shape, gain.dtype),
            pltpu.SemaphoreType.DMA((4,)),
        ],
        compiler_params=pltpu.CompilerParams(vmem_limit_bytes=VMEM_LIMIT),
        name="pick_rows",
    )(*(in_hbm(array) for array in (ids, gate_vals, tokens, gain)))


def expert_rows(rows, gate_ref, up_ref, down_ref):
    dims = (((1,), (1,)), ((), ()))
    gate_act = lax.dot_general(rows, gate_ref[...], dims, preferred_element_type=jnp.float32)
    up_act = lax.dot_general(rows, up_ref[...], dims, preferred_element_type=jnp.float32)
    hidden = (jax.nn.silu(gate_act) * up_act).astype(jnp.bfloat16)
    partial_out = jnp.dot(hidden, down_ref[...], preferred_element_type=jnp.float32)
    return partial_out.astype(jnp.bfloat16)


def expert_blocks(ins, weights, outs):
    together = max(1, 128 // ins[0].shape[0])
    for first in range(0, len(ins), together):
        some = ins[first : first + together]
        partial_out = expert_rows(jnp.concatenate([ref[...] for ref in some], axis=0), *weights)
        at = 0
        for ref in outs[first : first + together]:
            ref[...] = partial_out[at : at + ref.shape[0]]
            at += ref.shape[0]


def expert_cost(blocks, weights):
    size = sum(weight.size for weight in weights)
    rows = sum(block.shape[0] for block in blocks)
    return pl.CostEstimate(flops=2 * rows * size, bytes_accessed=2 * size, transcendentals=0)


def chunk_copies(source, target, chunks, sems):
    rows = source.shape[0] // chunks
    for i in range(chunks):
        at = pl.ds(i * rows, rows)
        yield pltpu.make_async_copy(source.at[at], target.at[at], sems.at[i])


def stage_kernel(live_ref, rows_ref, table_ref, *refs):
    *refs, sems = refs
    sources, (rows_out, table_out), weights = refs[:3], refs[3:5], refs[5:]
    copies = [
        copy
        for i, pair in enumerate(zip(sources, weights))
        for copy in chunk_copies(*pair, WEIGHT_CHUNKS, sems.at[i])
    ]
    for copy in copies:
        copy.start()
    rows_out[...] = rows_ref[...]
    token = lax.broadcasted_iota(jnp.int32, table_ref.shape, 1)
    table = jnp.where(token < live_ref[0], table_ref[...], 0.0)
    pieces = []
    for _ in range(3):
        pieces.append(table.astype(jnp.bfloat16).astype(jnp.float32))
        table = table - pieces[-1]
    table_out[...] = jnp.concatenate(pieces, axis=0).T.astype(jnp.bfloat16)
    for copy in copies:
        copy.wait()


def stage_weights(live_counts, rows, table, weights):
    vmem = pl.BlockSpec(memory_space=pltpu.VMEM)
    hbm = pl.BlockSpec(memory_space=pltpu.HBM)
    table_shape = (table.shape[1], 3 * table.shape[0])
    rows, table, *weights = pl.pallas_call(
        stage_kernel,
        out_shape=[
            jax.ShapeDtypeStruct(shape, jnp.bfloat16)
            for shape in (rows.shape, table_shape, *(weight.shape for weight in weights))
        ],
        in_specs=[pl.BlockSpec(memory_space=pltpu.SMEM), vmem, vmem] + [hbm] * 3,
        out_specs=[vmem] * 5,
        scratch_shapes=[pltpu.SemaphoreType.DMA((3, WEIGHT_CHUNKS))],
        compiler_params=pltpu.CompilerParams(vmem_limit_bytes=VMEM_LIMIT),
        cost_estimate=expert_cost([rows], weights),
        name="stage_weights",
    )(live_counts, rows, table, *(in_hbm(weight) for weight in weights))
    return rows, table, weights


def slice_kernel(count, *refs):
    outs = refs[len(refs) - count :]
    expert_blocks(refs[:count], refs[count : count + 3], outs)


def expert_slice(blocks, weights, after=()):
    vmem = pl.BlockSpec(memory_space=pltpu.VMEM)
    count = len(blocks)
    return pl.pallas_call(
        functools.partial(slice_kernel, count),
        out_shape=[jax.ShapeDtypeStruct(block.shape, jnp.bfloat16) for block in blocks],
        in_specs=[vmem] * (count + 3) + [pl.BlockSpec(memory_space=pl.ANY)] * len(after),
        out_specs=[vmem] * count,
        compiler_params=pltpu.CompilerParams(vmem_limit_bytes=VMEM_LIMIT),
        cost_estimate=expert_cost(blocks, weights),
        name="expert_slice",
    )(*blocks, *weights, *after)


def add_level(kept, came):
    return (kept.astype(jnp.float32) + came.astype(jnp.float32)).astype(jnp.bfloat16)


def combine_kernel(table_ref, *refs):
    *parts, out_hbm, out_ref, sems = refs
    features = out_ref.shape[1]
    width = features // 4
    copies = []
    for i in range(4):
        columns = pl.ds(i * width, width)
        summed = functools.reduce(add_level, [part[:, columns] for part in parts])
        result = jnp.dot(
            table_ref[...],
            jnp.concatenate([summed] * 3, axis=0),
            preferred_element_type=jnp.float32,
        )
        out_ref[:, columns] = result.astype(jnp.bfloat16)
        copies.append(
            pltpu.make_async_copy(out_ref.at[:, columns], out_hbm.at[:, columns], sems.at[i])
        )
        copies[-1].start()
    for copy in copies:
        copy.wait()


def combine(table, parts):
    vmem = pl.BlockSpec(memory_space=pltpu.VMEM)
    shape = (table.shape[0], parts[0].shape[1])
    return pl.pallas_call(
        combine_kernel,
        out_shape=jax.ShapeDtypeStruct(shape, jnp.bfloat16),
        in_specs=[vmem] * (1 + len(parts)),
        out_specs=pl.BlockSpec(memory_space=pltpu.HBM),
        scratch_shapes=[pltpu.VMEM(shape, jnp.bfloat16), pltpu.SemaphoreType.DMA((4,))],
        compiler_params=pltpu.CompilerParams(vmem_limit_bytes=VMEM_LIMIT),
        name="combine",
    )(table, *parts)


def across_groups(flight, blocks):
    if flight == 1:
        return blocks
    groups = [[g * SLICES + m for g in range(flight)] for m in range(SLICES)]
    return lax.all_to_all(
        blocks, "ep", split_axis=0, concat_axis=0, axis_index_groups=groups, tiled=True
    )


def swap(devices, distance, block):
    return lax.ppermute(block, "ep", [(i, i ^ distance) for i in range(devices)])


def on_device(tokens, norm_gain, expert_ids, gate_vals, live_counts, w_gate, w_up, w_down):
    features = tokens.shape[1]
    devices = lax.axis_size("ep")
    flight = devices // SLICES
    slots = flight * CAP
    rows, table = pick_rows(
        slots, expert_ids.T, gate_vals.T, tokens, norm_gain.reshape(1, features)
    )
    own = across_groups(flight, rows)
    farther, far = swap(devices, 6, own), swap(devices, 4, own)
    own, table, weights = stage_weights(live_counts, own, table, (w_gate.T, w_up.T, w_down))
    near = swap(devices, 2, own)
    outer, inner = jnp.concatenate([far, farther]), jnp.concatenate([own, near])
    outer_y, inner_y = swap(devices, 1, outer), swap(devices, 1, inner)
    (outer_y,) = expert_slice((outer_y,), weights)
    outer, inner, inner_y = expert_slice((outer, inner, inner_y), weights, (outer_y,))
    farther_y, far_y = swap(devices, 1, outer_y[slots:]), swap(devices, 1, outer_y[:slots])
    inner_y = swap(devices, 1, inner_y)
    far, farther = add_level(outer[:slots], far_y), add_level(outer[slots:], farther_y)
    own, near = (add_level(inner[at], inner_y[at]) for at in (slice(slots), slice(slots, None)))
    farther, far = swap(devices, 6, farther), swap(devices, 4, far)
    parts = [own, swap(devices, 2, near), add_level(far, farther)]
    if flight > 1:
        parts = [across_groups(flight, functools.reduce(add_level, parts))]
    return combine(table, parts)


def solution(mesh):
    return jax.shard_map(
        on_device,
        mesh=mesh,
        in_specs=(
            P(("sp", "ep"), None),
            P(),
            P(("sp", "ep"), None),
            P(("sp", "ep"), None),
            P(("sp", "ep")),
            P(None, "ep"),
            P(None, "ep"),
            P("ep", None),
        ),
        out_specs=P(("sp", "ep"), None),
        check_vma=False,
    )
```
